512 devices in a mesh: ctx: 64 (over y, z_lo, x), head: 8 (over z_hi, core).
Axes of the slice: x: 4, y: 8, z: 8 (z_hi: 4, z_lo: 2; z = z_hi * 2 + z_lo), core: 2. Of those that a mesh axis runs over, the one named last changes fastest.
Arguments:
- queries: bfloat16 [8192, 8192], P(('ctx', 'head')), may hold values from -8 to 8
- keys: bfloat16 [8192, 1024], P(('ctx', 'head')), may hold values from -8 to 8
- values: bfloat16 [8192, 1024], P(('ctx', 'head')), may hold values from -6 to 6
- output_gradient: bfloat16 [8192, 8192], P('ctx', 'head'), may hold values from -6 to 6
- segment_ids: int32 [8192], replicated, may hold values from 0 to 23, never falling along the last dimension, each value on 1 to 512 neighbouring positions
- block_order: int32 [128], replicated, may hold values from 0 to 127, each once
Outputs:
- attended: bfloat16 [8192, 8192], P('ctx', 'head')
- grad_queries: bfloat16 [8192, 8192], P(('ctx', 'head'))
- key_gradient: bfloat16 [8192, 1024], P(('ctx', 'head'))
- value_gradient: bfloat16 [8192, 1024], P(('ctx', 'head'))
The draws below stay inside these ranges and needn't reach their ends.
Inputs may be any that keep to these rules, and one draw needn't show every extreme that they name: `segment_ids`: labels never fall along the sequence; each rollout holds 1 to 512 positions and one holds exactly 512. `block_order`: each of the 128 sequence blocks is held once.
All inputs are finite; a program needn't handle non-finite values.
Results may differ from the reference program's by a relative error of at most 0.035.
Values may be sent and summed in bfloat16 or wider, within the bound.
A program may use at most 64 MiB of HBM per device.

```python
import math
import jax
import jax.numpy as jnp
import numpy as np
from jax import lax

QUERY_HEADS = 64
KEY_VALUE_HEADS = 8
HEAD_SPAN = 128
DOC_MOST = 512
PACKED_TOKENS = 8192
HALF = 64
DOCS = 24
N_CTX = 64


def draw_queries(key, part):
    key = jax.random.fold_in(key, 11)
    sampled = jax.random.normal(key, (PACKED_TOKENS, QUERY_HEADS, HEAD_SPAN), jnp.float32)
    return sampled.reshape(PACKED_TOKENS, QUERY_HEADS * HEAD_SPAN).astype(jnp.bfloat16)


def draw_keys(key, part):
    key = jax.random.fold_in(key, 17)
    sampled = jax.random.normal(key, (PACKED_TOKENS, KEY_VALUE_HEADS, HEAD_SPAN), jnp.float32)
    return sampled.reshape(PACKED_TOKENS, KEY_VALUE_HEADS * HEAD_SPAN).astype(jnp.bfloat16)


def block_scale(key, shape, split, low, high):
    loudness, own = 1.0, jax.random.fold_in(key, 6)
    for dim, shards_of in split:
        heights = jnp.exp(jax.random.uniform(jax.random.fold_in(own, dim), (shards_of,), jnp.float32, low / len(split), high / len(split)))
        loudness = loudness * jnp.repeat(heights, shape[dim] // shards_of).reshape([-1 if axis == dim else 1 for axis in range(len(shape))])
    return loudness


def split_up(count, total, limit, skew):
    loads = [(1 << 20) // math.isqrt(grade ** skew) + 1 for grade in range(2, count + 1)]
    spare, holding = total - limit - (count - 1), [1] * (count - 1)
    while spare > 0:
        candidates = [i for i in range(count - 1) if holding[i] < limit]
        whole, remaining = sum([loads[i] for i in candidates]), spare
        for i in candidates:
            extra = min(limit - holding[i], max(1, remaining * loads[i] // whole), spare)
            holding[i] = holding[i] + extra
            spare = spare - extra
    return np.array([limit] + holding)


def uneven(own_key, count, total, bound, lean):
    if count == 2:
        one = jax.random.randint(own_key, (), max(1, total - bound), min(bound, total - 1) + 1)
        return jnp.stack([one, total - one])
    lengths = jnp.asarray(split_up(count, total, bound, lean), jnp.int32)
    twos = (count - 1) // 2
    donor, receiver = lengths[1:1 + 2 * twos:2], lengths[2:2 + 2 * twos:2]
    room = jnp.minimum(donor - 1, bound - receiver)
    passed = jax.random.randint(jax.random.fold_in(own_key, 1), (twos,), 0, 1 << 20) % (room + 1)
    lengths = lengths.at[1:1 + 2 * twos:2].set(donor - passed).at[2:2 + 2 * twos:2].set(receiver + passed)
    return lengths[jax.random.permutation(jax.random.fold_in(own_key, 2), count)]


def scatter_about(rng, shape, scale, bound, pieces=(), kind=jnp.bfloat16):
    result = scale * jax.random.normal(rng, shape, jnp.float32)
    if pieces:
        result = result * block_scale(rng, shape, pieces, -0.22, 0.18)
    return jnp.clip(result, -bound, bound).astype(kind)


def setup_inputs(seed: int = 0) -> dict:
    streams_of = jax.random.split(jax.random.key(seed), 7)
    return {
        "queries": draw_queries(jax.random.fold_in(streams_of[6], 71), 0),
        "keys": draw_keys(jax.random.fold_in(streams_of[6], 71), 0),
        "values": scatter_about(streams_of[2], (PACKED_TOKENS, KEY_VALUE_HEADS * HEAD_SPAN), 1.0, 6.0, ((0, 512),)),
        "output_gradient": scatter_about(streams_of[3], (PACKED_TOKENS, QUERY_HEADS * HEAD_SPAN), 1.0, 6.0, ((0, 64), (1, 8))),
        "segment_ids": jnp.searchsorted(jnp.cumsum(uneven(streams_of[4], DOCS, PACKED_TOKENS, DOC_MOST, 1)), jnp.arange(PACKED_TOKENS), side="right").astype(jnp.int32),
        "block_order": jax.random.permutation(streams_of[5], 2 * N_CTX).astype(jnp.int32),
    }


masked_score = -1.0e30


def round_half(value):
    return lax.optimization_barrier(value.astype(jnp.bfloat16)).astype(jnp.float32)


def reference(queries, keys, values, output_gradient, segment_ids, block_order):
    group_count = QUERY_HEADS // KEY_VALUE_HEADS
    score_scale = HEAD_SPAN ** -0.5
    slot_count = 2 * N_CTX
    where_block = jnp.zeros((slot_count,), jnp.int32).at[block_order].set(jnp.arange(slot_count, dtype=jnp.int32))

    def into_token_order(array):
        return array.reshape(slot_count, HALF, array.shape[1])[where_block].reshape(PACKED_TOKENS, array.shape[1])

    def to_storage(array):
        return array.reshape(slot_count, HALF, array.shape[1])[block_order].reshape(PACKED_TOKENS, array.shape[1])

    sequence_queries = into_token_order(queries).reshape(PACKED_TOKENS, KEY_VALUE_HEADS, group_count, HEAD_SPAN).transpose(1, 0, 2, 3)
    sequence_keys = into_token_order(keys).reshape(PACKED_TOKENS, KEY_VALUE_HEADS, HEAD_SPAN).transpose(1, 0, 2)
    sequence_values = into_token_order(values).reshape(PACKED_TOKENS, KEY_VALUE_HEADS, HEAD_SPAN).transpose(1, 0, 2)
    gradient_sequence = into_token_order(output_gradient).reshape(PACKED_TOKENS, KEY_VALUE_HEADS, group_count, HEAD_SPAN).transpose(1, 0, 2, 3)
    window = DOC_MOST + HALF
    block_total = PACKED_TOKENS // HALF
    pad_labels = jnp.concatenate([jnp.full((DOC_MOST,), -1, jnp.int32), segment_ids])
    pad_places = jnp.arange(PACKED_TOKENS + DOC_MOST, dtype=jnp.int32) - DOC_MOST
    highest = lax.Precision.HIGHEST

    def one_head(operands):
        query_head, key_head, value_head, grad_head = operands
        key_pad = jnp.concatenate([jnp.zeros((DOC_MOST, HEAD_SPAN), key_head.dtype), key_head])
        value_pad = jnp.concatenate([jnp.zeros((DOC_MOST, HEAD_SPAN), value_head.dtype), value_head])

        def visit(carry, index):
            key_accum, value_accum = carry
            first = index * HALF
            query_block = lax.dynamic_slice_in_dim(query_head, first, HALF).astype(jnp.float32)
            grad_block = lax.dynamic_slice_in_dim(grad_head, first, HALF).astype(jnp.float32)
            key_window = lax.dynamic_slice_in_dim(key_pad, first, window).astype(jnp.float32)
            value_window = lax.dynamic_slice_in_dim(value_pad, first, window).astype(jnp.float32)
            query_labels = lax.dynamic_slice_in_dim(segment_ids, first, HALF)
            query_places = first + jnp.arange(HALF, dtype=jnp.int32)
            key_labels = lax.dynamic_slice_in_dim(pad_labels, first, window)
            key_places = lax.dynamic_slice_in_dim(pad_places, first, window)
            allowed = (query_labels[:, None] == key_labels[None, :]) & (key_places[None, :] <= query_places[:, None])
            allowed = allowed[:, None, :]
            scores = jnp.einsum("tgd,kd->tgk", query_block, key_window, precision=highest) * score_scale
            scores = jnp.where(allowed, scores, masked_score)
            top = jnp.max(scores, axis=-1, keepdims=True)
            raised = jnp.where(allowed, jnp.exp(scores - top), 0.0)
            total = jnp.sum(raised, axis=-1, keepdims=True)
            weights = round_half(raised)
            attended_block = (jnp.einsum("tgk,kd->tgd", weights, value_window, precision=highest) / total).astype(jnp.bfloat16)
            attended_wide = attended_block.astype(jnp.float32)
            dsum = jnp.sum(grad_block * attended_wide, axis=-1, keepdims=True)
            probs = raised / total
            probs_b = round_half(probs)
            value_part = jnp.einsum("tgk,tgd->kd", probs_b, grad_block, precision=highest)
            dprobs = jnp.einsum("tgd,kd->tgk", grad_block, value_window, precision=highest)
            dscores = round_half(probs * (dprobs - dsum))
            query_grad = score_scale * jnp.einsum("tgk,kd->tgd", dscores, key_window, precision=highest)
            key_part = score_scale * jnp.einsum("tgk,tgd->kd", dscores, query_block, precision=highest)
            key_accum = lax.dynamic_update_slice_in_dim(key_accum, lax.dynamic_slice_in_dim(key_accum, first, window) + key_part, first, 0)
            value_accum = lax.dynamic_update_slice_in_dim(value_accum, lax.dynamic_slice_in_dim(value_accum, first, window) + value_part, first, 0)
            return (key_accum, value_accum), (attended_block, query_grad)

        zeros_pad = jnp.zeros((PACKED_TOKENS + DOC_MOST, HEAD_SPAN), jnp.float32)
        (key_accum, value_accum), (attended_blocks, query_grads) = lax.scan(visit, (zeros_pad, zeros_pad), jnp.arange(block_total, dtype=jnp.int32))
        return (attended_blocks.reshape(PACKED_TOKENS, group_count, HEAD_SPAN), query_grads.reshape(PACKED_TOKENS, group_count, HEAD_SPAN), key_accum[DOC_MOST:], value_accum[DOC_MOST:])

    attended_heads, query_heads, head_keys, head_values = lax.map(one_head, (sequence_queries, sequence_keys, sequence_values, gradient_sequence))
    attended = attended_heads.transpose(1, 0, 2, 3).reshape(PACKED_TOKENS, QUERY_HEADS * HEAD_SPAN)
    grad_queries = query_heads.transpose(1, 0, 2, 3).reshape(PACKED_TOKENS, QUERY_HEADS * HEAD_SPAN).astype(jnp.bfloat16)
    key_gradient = head_keys.transpose(1, 0, 2).reshape(PACKED_TOKENS, KEY_VALUE_HEADS * HEAD_SPAN).astype(jnp.bfloat16)
    value_gradient = head_values.transpose(1, 0, 2).reshape(PACKED_TOKENS, KEY_VALUE_HEADS * HEAD_SPAN).astype(jnp.bfloat16)
    return (to_storage(attended), to_storage(grad_queries), to_storage(key_gradient), to_storage(value_gradient))
```

```python
import functools

import jax
import jax.numpy as jnp
import numpy as np
from jax import lax
from jax.experimental import pallas as pl
from jax.experimental.pallas import tpu as pltpu
from jax.sharding import PartitionSpec as P

SPAN = 128
BLOCK = 64
GROUP = 8
BACK = 8
SEEN = BACK + 1
WINDOW = SEEN * BLOCK
LINE = 4
PAIR = 2
CLASSES = 16
PIECES = 8
PART = SEEN * 8
LANES = 256
NEVER = -1e30

MESH = pl.DeviceIdType.MESH
NT = (((1,), (1,)), ((), ()))
TN = (((0,), (0,)), ((), ()))


def rank_of(c):
    return (lax.rem(c // LINE, PAIR)) * PIECES + lax.rem(c // (LINE * PAIR), 2) * LINE + lax.rem(c, LINE)


def member(c, e):
    x = lax.rem(lax.rem(c, LINE) + lax.rem(e, LINE), LINE)
    z = lax.rem(lax.rem(c // LINE, PAIR) + lax.rem(e // LINE, PAIR), PAIR)
    y = lax.rem(lax.rem(c // (LINE * PAIR), 2) + e // (LINE * PAIR), 2)
    return (c // CLASSES) * CLASSES + (y * PAIR + z) * LINE + x


def await_bytes(ref, sem):
    pltpu.make_async_copy(ref, ref, sem).wait()


def kernel(
    nc, nh,
    order, place, q_ref, k_ref, v_ref, do_ref, seg_ref,
    att_out, dq_out, dk_out, dv_out,
    q_loc, kv_loc, spread, r1, stored, seq, s2, r2, keys, vals, dot_t, bias,
    probs, dscores, dq_loc, s3, r3, r3f, acc, s4, r4, dkv_loc,
    send_sem, recv_sem,
):
    c = lax.axis_index("ctx")
    h = lax.axis_index("head")
    rows = q_ref.shape[0]
    wide = GROUP * SPAN
    blocks = 2 * nc
    f32, bf16 = jnp.float32, jnp.bfloat16

    def remote(src, dst, which, where):
        return pltpu.make_async_remote_copy(
            src_ref=src, dst_ref=dst, send_sem=send_sem.at[which], recv_sem=recv_sem.at[which],
            device_id=where, device_id_type=MESH,
        )

    barrier = pltpu.get_barrier_semaphore()

    def greet_ctx(d, _):
        pl.semaphore_signal(barrier, inc=1, device_id={"ctx": lax.rem(c + d, nc)}, device_id_type=MESH)
        return 0

    def greet_head(d, _):
        pl.semaphore_signal(barrier, inc=1, device_id={"head": lax.rem(h + d, nh)}, device_id_type=MESH)
        return 0

    lax.fori_loop(1, nh, greet_head, 0)
    lax.fori_loop(1, nc, greet_ctx, 0)
    pl.semaphore_wait(barrier, nc - 1 + nh - 1)

    def own_rows(g):
        return pl.ds(pl.multiple_of(g * rows, rows), rows)

    def head_columns(g, width):
        return pl.ds(pl.multiple_of(g * width, width), width)

    def send_kv(d, _):
        g = lax.rem(h + d, nh)
        remote(k_ref.at[:, head_columns(g, SPAN)], kv_loc.at[0, own_rows(h), :], 0, {"head": g}).start()
        remote(v_ref.at[:, head_columns(g, SPAN)], kv_loc.at[1, own_rows(h), :], 0, {"head": g}).start()
        return 0

    lax.fori_loop(1, nh, send_kv, 0)
    kv_loc[0, own_rows(h), :] = k_ref[:, head_columns(h, SPAN)]
    kv_loc[1, own_rows(h), :] = v_ref[:, head_columns(h, SPAN)]
    if nh > 1:
        await_bytes(kv_loc.at[:, pl.ds(0, (nh - 1) * rows), :], recv_sem.at[0])

    for kind in range(2):
        whole = kv_loc[kind].astype(f32)
        for piece in range(PIECES):
            upper = whole[piece * 8 : piece * 8 + 8]
            lower = whole[BLOCK + piece * 8 : BLOCK + piece * 8 + 8]
            spread[kind * PIECES + piece] = jnp.concatenate([upper, lower], axis=0).astype(bf16)

    def send_spread(d, _):
        j = lax.rem(c + d, nc)
        remote(spread.at[rank_of(j)], r1.at[c], 1, {"ctx": j}).start()
        return 0

    lax.fori_loop(1, nc, send_spread, 0)
    r1[c] = spread[rank_of(c)]

    def send_q(d, _):
        g = lax.rem(h + d, nh)
        remote(q_ref.at[:, head_columns(g, wide)], q_loc.at[own_rows(h), :], 2, {"head": g}).start()
        return 0

    lax.fori_loop(1, nh, send_q, 0)
    q_loc[own_rows(h), :] = q_ref[:, head_columns(h, wide)]

    lane = lax.broadcasted_iota(jnp.int32, (SPAN, SPAN), 1)
    diagonal = lane == lax.broadcasted_iota(jnp.int32, (SPAN, SPAN), 0)
    first_half = lane[:1] < BLOCK
    b0, b1 = order[2 * c], order[2 * c + 1]
    line0 = seg_ref[pl.ds(b0 // 2, 1), :]
    line1 = seg_ref[pl.ds(b1 // 2, 1), :]
    line0 = jnp.where(lax.rem(b0, 2) == 0, line0, jnp.concatenate([line0[:, BLOCK:], line0[:, :BLOCK]], axis=1))
    line1 = jnp.where(lax.rem(b1, 2) == 1, line1, jnp.concatenate([line1[:, BLOCK:], line1[:, :BLOCK]], axis=1))
    label_row = jnp.where(first_half, line0, line1)
    label_col = jnp.sum(jnp.where(diagonal, label_row, 0), axis=1, keepdims=True)

    def count_lower(r, count):
        return count + jnp.where(seg_ref[pl.ds(r, 1), :] < label_col, 1, 0)

    count = lax.fori_loop(0, nc, count_lower, jnp.zeros((SPAN, SPAN), jnp.int32))
    start_col = jnp.sum(count, axis=1, keepdims=True)
    start_row = jnp.sum(jnp.where(diagonal, start_col, 0), axis=0, keepdims=True)
    swapped = jnp.concatenate([start_row[:, BLOCK:], start_row[:, :BLOCK]], axis=1)
    shape4 = (PIECES, SEEN, 8, SPAN)
    key_place = (
        lax.broadcasted_iota(jnp.int32, shape4, 0) * 8
        + lax.broadcasted_iota(jnp.int32, shape4, 1) * BLOCK
        + lax.broadcasted_iota(jnp.int32, shape4, 2)
    ).reshape(WINDOW, SPAN)
    high = BACK * BLOCK + jnp.where(first_half, lane[:1], lane[:1] - BLOCK)
    for i, b in enumerate((b0, b1)):
        both = jnp.where(first_half, start_row, swapped) if i == 0 else jnp.where(first_half, swapped, start_row)
        low = both - (b - BACK) * BLOCK
        bias[i] = jnp.where((key_place >= low) & (key_place <= high), 0.0, NEVER)

    for i in range(2):
        for head in range(GROUP):
            part = do_ref[i * BLOCK : (i + 1) * BLOCK, head * SPAN : (head + 1) * SPAN].astype(f32)
            dot_t[i, :, head * BLOCK : (head + 1) * BLOCK] = part.T

    await_bytes(r1.at[pl.ds(0, nc - 1)], recv_sem.at[1])
    stored[...] = r1[...].astype(f32).reshape(blocks, 8, SPAN)
    seq[pl.ds(0, BACK)] = jnp.zeros((BACK, 8, SPAN), f32)

    def to_sequence(b, _):
        seq[b + BACK] = stored[place[b]]
        return 0

    lax.fori_loop(0, blocks, to_sequence, 0, unroll=8)

    def windows_of(j):
        both = [seq[pl.ds(order[2 * j + i], SEEN)] for i in range(2)]
        return jnp.concatenate(both, axis=0).reshape(2 * PART, SPAN).astype(bf16)

    def send_windows(e, _):
        j = member(c, e)
        s2[e] = windows_of(j)
        remote(s2.at[e], r2.at[rank_of(c)], 3, {"ctx": j}).start()
        return 0

    lax.fori_loop(1, CLASSES, send_windows, 0)
    r2[rank_of(c)] = windows_of(c)
    await_bytes(r2.at[pl.ds(0, CLASSES - 1)], recv_sem.at[3])
    for kind, target in enumerate((keys, vals)):
        for i in range(2):
            for piece in range(PIECES):
                both = r2[kind * PIECES + piece].astype(f32)
                target[i, piece * PART : (piece + 1) * PART, :] = both[i * PART : (i + 1) * PART]
    if nh > 1:
        await_bytes(q_loc.at[pl.ds(0, (nh - 1) * rows), :], recv_sem.at[2])

    scale = SPAN ** (-0.5)
    power = scale * float(np.log2(np.e))
    key_grads, value_grads = [], []
    for i in range(2):
        key_tile, value_tile = keys[i].astype(bf16), vals[i].astype(bf16)
        block = pl.ds(i * BLOCK, BLOCK)
        for part in range(GROUP * BLOCK // LANES):
            heads = range(part * LANES // BLOCK, (part + 1) * LANES // BLOCK)
            lanes = slice(part * LANES, (part + 1) * LANES)
            query = jnp.concatenate([q_loc[block, a * SPAN : (a + 1) * SPAN] for a in heads], axis=0)
            cotangent = jnp.concatenate([do_ref[block, a * SPAN : (a + 1) * SPAN] for a in heads], axis=0)
            scores = lax.dot_general(key_tile, query, NT, preferred_element_type=f32)
            scores = scores + jnp.concatenate([bias[i]] * (LANES // SPAN), axis=1)
            top = jnp.max(scores, axis=0, keepdims=True)
            raised = jnp.exp2((scores - top) * power)
            total = jnp.sum(raised, axis=0, keepdims=True)
            sums = lax.dot_general(value_tile, raised.astype(bf16), TN, preferred_element_type=f32)
            inverse = 1.0 / total
            attended = (sums * inverse).astype(bf16).astype(f32)
            dsum = jnp.sum(dot_t[i, :, lanes] * attended, axis=0, keepdims=True)
            prob = raised * inverse
            probs[:, lanes] = prob.astype(bf16)
            dprob = lax.dot_general(value_tile, cotangent, NT, preferred_element_type=f32)
            dscore = (prob * (dprob - dsum)).astype(bf16)
            dscores[:, lanes] = dscore
            query_grad = lax.dot_general(key_tile, dscore, TN, preferred_element_type=f32) * scale
            attended_rows = attended.T.astype(bf16)
            query_grad_rows = query_grad.T.astype(bf16)
            for n, a in enumerate(heads):
                att_out[block, a * SPAN : (a + 1) * SPAN] = attended_rows[n * BLOCK : (n + 1) * BLOCK]
                dq_loc[block, a * SPAN : (a + 1) * SPAN] = query_grad_rows[n * BLOCK : (n + 1) * BLOCK]
        query = jnp.concatenate([q_loc[block, a * SPAN : (a + 1) * SPAN] for a in range(GROUP)], axis=0)
        cotangent = jnp.concatenate([do_ref[block, a * SPAN : (a + 1) * SPAN] for a in range(GROUP)], axis=0)
        keys[i] = jnp.dot(dscores[...], query, preferred_element_type=f32) * scale
        vals[i] = jnp.dot(probs[...], cotangent, preferred_element_type=f32)

    for kind, source in enumerate((keys, vals)):
        for piece in range(PIECES):
            both = [source[i, piece * PART : (piece + 1) * PART, :] for i in range(2)]
            s3[kind * PIECES + piece] = jnp.concatenate(both, axis=0).astype(bf16)

    def send_back(e, _):
        j = member(c, e)
        remote(s3.at[rank_of(j)], r3.at[rank_of(c)], 4, {"ctx": j}).start()
        return 0

    lax.fori_loop(1, CLASSES, send_back, 0)
    r3[rank_of(c)] = s3[rank_of(c)]

    def send_dq(d, _):
        g = lax.rem(h + d, nh)
        remote(dq_loc.at[own_rows(g), :], dq_out.at[:, head_columns(h, wide)], 5, {"head": g}).start()
        return 0

    lax.fori_loop(1, nh, send_dq, 0)
    dq_out[:, head_columns(h, wide)] = dq_loc[own_rows(h), :]

    await_bytes(r3.at[pl.ds(0, CLASSES - 1)], recv_sem.at[4])
    r3f[pl.ds(0, 2 * CLASSES)] = r3[...].astype(f32).reshape(2 * CLASSES, SEEN, 8, SPAN)
    r3f[2 * CLASSES] = jnp.zeros((SEEN, 8, SPAN), f32)

    def add_up(b, sums):
        s = place[b]
        j = s // 2
        slot = jnp.where(j // CLASSES == c // CLASSES, rank_of(j) * 2 + lax.rem(s, 2), 2 * CLASSES)
        new = r3f[slot]
        sums = [sums[k] + new[k] for k in range(SEEN)]
        acc[b] = sums[0]
        return tuple(sums[1:]) + (jnp.zeros((8, SPAN), f32),)

    sums = lax.fori_loop(0, blocks, add_up, tuple(jnp.zeros((8, SPAN), f32) for _ in range(SEEN)), unroll=4)
    for k in range(BACK):
        acc[blocks + k] = sums[k]

    def tile_of(j):
        both = [acc[order[2 * j + i] + BACK] for i in range(2)]
        return jnp.concatenate(both, axis=0).astype(bf16)

    def send_sums(d, _):
        j = lax.rem(c + d, nc)
        s4[j] = tile_of(j)
        remote(s4.at[j], r4.at[c], 6, {"ctx": j}).start()
        return 0

    lax.fori_loop(1, nc, send_sums, 0)
    r4[c] = tile_of(c)
    await_bytes(r4.at[pl.ds(0, nc - 1)], recv_sem.at[6])
    for kind in range(2):
        uppers, lowers = [], []
        for piece in range(PIECES):
            base = (piece // LINE) * LINE * PAIR + kind * LINE + piece % LINE
            tile = r4[base].astype(f32)
            for copy in range(1, nc // CLASSES):
                tile = tile + r4[copy * CLASSES + base].astype(f32)
            uppers.append(tile[:8])
            lowers.append(tile[8:])
        dkv_loc[kind] = jnp.concatenate(uppers + lowers, axis=0).astype(bf16)

    def send_dkv(d, _):
        g = lax.rem(h + d, nh)
        remote(dkv_loc.at[0, own_rows(g), :], dk_out.at[:, head_columns(h, SPAN)], 7, {"head": g}).start()
        remote(dkv_loc.at[1, own_rows(g), :], dv_out.at[:, head_columns(h, SPAN)], 7, {"head": g}).start()
        return 0

    lax.fori_loop(1, nh, send_dkv, 0)
    dk_out[:, head_columns(h, SPAN)] = dkv_loc[0, own_rows(h), :]
    dv_out[:, head_columns(h, SPAN)] = dkv_loc[1, own_rows(h), :]

    some = pl.ds(0, (nh - 1) * rows)
    if nh > 1:
        await_bytes(q_loc.at[some, :], recv_sem.at[5])
        await_bytes(kv_loc.at[:, some, :], recv_sem.at[7])
        await_bytes(kv_loc.at[:, some, :], send_sem.at[0])
        await_bytes(q_loc.at[some, :], send_sem.at[2])
        await_bytes(q_loc.at[some, :], send_sem.at[5])
        await_bytes(kv_loc.at[:, some, :], send_sem.at[7])
    await_bytes(r1.at[pl.ds(0, nc - 1)], send_sem.at[1])
    await_bytes(r2.at[pl.ds(0, CLASSES - 1)], send_sem.at[3])
    await_bytes(r3.at[pl.ds(0, CLASSES - 1)], send_sem.at[4])
    await_bytes(r4.at[pl.ds(0, nc - 1)], send_sem.at[6])


def shards(queries, keys, values, output_gradient, segment_ids, block_order):
    nc, nh = lax.axis_size("ctx"), lax.axis_size("head")
    rows, wide, blocks = queries.shape[0], GROUP * SPAN, 2 * nc
    spots = jnp.arange(blocks, dtype=jnp.int32)
    place = jnp.sum(jnp.where(block_order[None, :] == spots[:, None], spots[None, :], 0), axis=1, dtype=jnp.int32)
    bf16, f32 = jnp.bfloat16, jnp.float32
    vmem = pl.BlockSpec(memory_space=pltpu.VMEM)
    smem = pl.BlockSpec(memory_space=pltpu.SMEM)
    return pl.pallas_call(
        functools.partial(kernel, nc, nh),
        out_shape=(
            jax.ShapeDtypeStruct((2 * BLOCK, wide), bf16),
            jax.ShapeDtypeStruct(queries.shape, bf16),
            jax.ShapeDtypeStruct(keys.shape, bf16),
            jax.ShapeDtypeStruct(values.shape, bf16),
        ),
        in_specs=[smem, smem, vmem, vmem, vmem, vmem, vmem],
        out_specs=(vmem, vmem, vmem, vmem),
        scratch_shapes=[
            pltpu.VMEM((2 * BLOCK, wide), bf16),
            pltpu.VMEM((2, 2 * BLOCK, SPAN), bf16),
            pltpu.VMEM((CLASSES, 16, SPAN), bf16),
            pltpu.VMEM((nc, 16, SPAN), bf16),
            pltpu.VMEM((blocks, 8, SPAN), f32),
            pltpu.VMEM((blocks + BACK, 8, SPAN), f32),
            pltpu.VMEM((CLASSES, 2 * PART, SPAN), bf16),
            pltpu.VMEM((CLASSES, 2 * PART, SPAN), bf16),
            pltpu.VMEM((2, WINDOW, SPAN), f32),
            pltpu.VMEM((2, WINDOW, SPAN), f32),
            pltpu.VMEM((2, SPAN, GROUP * BLOCK), f32),
            pltpu.VMEM((2, WINDOW, SPAN), f32),
            pltpu.VMEM((WINDOW, GROUP * BLOCK), bf16),
            pltpu.VMEM((WINDOW, GROUP * BLOCK), bf16),
            pltpu.VMEM((2 * BLOCK, wide), bf16),
            pltpu.VMEM((CLASSES, 2 * PART, SPAN), bf16),
            pltpu.VMEM((CLASSES, 2 * PART, SPAN), bf16),
            pltpu.VMEM((2 * CLASSES + 1, SEEN, 8, SPAN), f32),
            pltpu.VMEM((blocks + BACK, 8, SPAN), f32),
            pltpu.VMEM((nc, 16, SPAN), bf16),
            pltpu.VMEM((nc, 16, SPAN), bf16),
            pltpu.VMEM((2, 2 * BLOCK, SPAN), bf16),
            pltpu.SemaphoreType.DMA((8,)),
            pltpu.SemaphoreType.DMA((8,)),
        ],
        compiler_params=pltpu.CompilerParams(
            collective_id=0, has_side_effects=True, vmem_limit_bytes=48 * 1024 * 1024
        ),
    )(block_order, place, queries, keys, values, output_gradient, segment_ids.reshape(nc, 2 * BLOCK))


def solution(mesh):
    in_specs = (
        P(("ctx", "head"), None),
        P(("ctx", "head"), None),
        P(("ctx", "head"), None),
        P("ctx", "head"),
        P(),
        P(),
    )
    out_specs = (
        P("ctx", "head"),
        P(("ctx", "head"), None),
        P(("ctx", "head"), None),
        P(("ctx", "head"), None),
    )
    return jax.shard_map(shards, mesh=mesh, in_specs=in_specs, out_specs=out_specs, check_vma=False)
```

```python
import functools

import jax
import jax.numpy as jnp
import numpy as np
from jax import lax
from jax.experimental import pallas as pl
from jax.experimental.pallas import tpu as pltpu
from jax.sharding import PartitionSpec as P

SPAN = 128
BLOCK = 64
GROUP = 8
BACK = 8
SEEN = BACK + 1
WINDOW = SEEN * BLOCK
LINE = 4
PAIR = 2
CLASSES = 16
PIECES = 8
PART = SEEN * 8
LANES = 256
NEVER = -1e30

MESH = pl.DeviceIdType.MESH
NT = (((1,), (1,)), ((), ()))
TN = (((0,), (0,)), ((), ()))


def rank_of(c):
    return (lax.rem(c // LINE, PAIR)) * PIECES + lax.rem(c // (LINE * PAIR), 2) * LINE + lax.rem(c, LINE)


def member(c, e):
    x = lax.rem(lax.rem(c, LINE) + lax.rem(e, LINE), LINE)
    z = lax.rem(lax.rem(c // LINE, PAIR) + lax.rem(e // LINE, PAIR), PAIR)
    y = lax.rem(lax.rem(c // (LINE * PAIR), 2) + e // (LINE * PAIR), 2)
    return (c // CLASSES) * CLASSES + (y * PAIR + z) * LINE + x


def await_bytes(ref, sem):
    pltpu.make_async_copy(ref, ref, sem).wait()


def kernel(
    nc, nh,
    order_hbm, q_ref, k_ref, v_ref, do_hbm, seg_hbm,
    att_out, dq_out, dk_out, dv_out,
    q_loc, kv_loc, spread, r1, stored, seq, s2, r2, keys, vals, dot_t, bias,
    probs, dscores, dq_loc, s3, r3, r3f, acc, s4, r4, dkv_loc,
    do_ref, seg_ref, order_row, place_row, order, place,
    send_sem, recv_sem, local_sem,
):
    c = lax.axis_index("ctx")
    h = lax.axis_index("head")
    rows = q_ref.shape[0]
    wide = GROUP * SPAN
    blocks = 2 * nc
    f32, bf16 = jnp.float32, jnp.bfloat16

    def remote(src, dst, which, where):
        return pltpu.make_async_remote_copy(
            src_ref=src, dst_ref=dst, send_sem=send_sem.at[which], recv_sem=recv_sem.at[which],
            device_id=where, device_id_type=MESH,
        )

    barrier = pltpu.get_barrier_semaphore()

    def greet_ctx(d, _):
        pl.semaphore_signal(barrier, inc=1, device_id={"ctx": lax.rem(c + d, nc)}, device_id_type=MESH)
        return 0

    def greet_head(d, _):
        pl.semaphore_signal(barrier, inc=1, device_id={"head": lax.rem(h + d, nh)}, device_id_type=MESH)
        return 0

    lax.fori_loop(1, nh, greet_head, 0)
    lax.fori_loop(1, nc, greet_ctx, 0)

    def own_rows(g):
        return pl.ds(pl.multiple_of(g * rows, rows), rows)

    def head_columns(g, width):
        return pl.ds(pl.multiple_of(g * width, width), width)

    fetch_kv = [
        pltpu.make_async_copy(source.at[:, head_columns(h, SPAN)], kv_loc.at[kind, own_rows(h), :], local_sem.at[kind])
        for kind, source in enumerate((k_ref, v_ref))
    ]
    fetch_order = [
        pltpu.make_async_copy(order_hbm, order, local_sem.at[2]),
        pltpu.make_async_copy(order_hbm, order_row, local_sem.at[3]),
    ]
    fetch_rest = [
        pltpu.make_async_copy(seg_hbm, seg_ref, local_sem.at[4]),
        pltpu.make_async_copy(do_hbm, do_ref, local_sem.at[5]),
        pltpu.make_async_copy(q_ref.at[:, head_columns(h, wide)], q_loc.at[own_rows(h), :], local_sem.at[6]),
    ]
    for fetch in fetch_order + fetch_kv + fetch_rest:
        fetch.start()
    for fetch in fetch_order:
        fetch.wait()

    spot = lax.broadcasted_iota(jnp.int32, (blocks, blocks), 0)
    across = lax.broadcasted_iota(jnp.int32, (blocks, blocks), 1)
    order_col = jnp.sum(jnp.where(spot == across, order_row[...], 0), axis=1, keepdims=True)
    place_row[...] = jnp.max(jnp.where(order_col == across, spot, 0), axis=0, keepdims=True)
    fetch_place = pltpu.make_async_copy(place_row, place, local_sem.at[7])
    fetch_place.start()

    pl.semaphore_wait(barrier, nc - 1 + nh - 1)

    def send_kv(d, _):
        g = lax.rem(h + d, nh)
        remote(k_ref.at[:, head_columns(g, SPAN)], kv_loc.at[0, own_rows(h), :], 0, {"head": g}).start()
        remote(v_ref.at[:, head_columns(g, SPAN)], kv_loc.at[1, own_rows(h), :], 0, {"head": g}).start()
        return 0

    lax.fori_loop(1, nh, send_kv, 0)
    for fetch in fetch_kv:
        fetch.wait()
    if nh > 1:
        await_bytes(kv_loc.at[:, pl.ds(0, (nh - 1) * rows), :], recv_sem.at[0])

    for kind in range(2):
        whole = kv_loc[kind].astype(f32)
        for piece in range(PIECES):
            upper = whole[piece * 8 : piece * 8 + 8]
            lower = whole[BLOCK + piece * 8 : BLOCK + piece * 8 + 8]
            spread[kind * PIECES + piece] = jnp.concatenate([upper, lower], axis=0).astype(bf16)

    def send_spread(d, _):
        j = lax.rem(c + d, nc)
        remote(spread.at[rank_of(j)], r1.at[c], 1, {"ctx": j}).start()
        return 0

    lax.fori_loop(1, nc, send_spread, 0)
    r1[c] = spread[rank_of(c)]

    def send_q(d, _):
        g = lax.rem(h + d, nh)
        remote(q_ref.at[:, head_columns(g, wide)], q_loc.at[own_rows(h), :], 2, {"head": g}).start()
        return 0

    lax.fori_loop(1, nh, send_q, 0)
    for fetch in fetch_rest:
        fetch.wait()
    fetch_place.wait()

    lane = lax.broadcasted_iota(jnp.int32, (SPAN, SPAN), 1)
    diagonal = lane == lax.broadcasted_iota(jnp.int32, (SPAN, SPAN), 0)
    first_half = lane[:1] < BLOCK
    b0, b1 = order[0, 2 * c], order[0, 2 * c + 1]
    line0 = seg_ref[pl.ds(b0 // 2, 1), :]
    line1 = seg_ref[pl.ds(b1 // 2, 1), :]
    line0 = jnp.where(lax.rem(b0, 2) == 0, line0, jnp.concatenate([line0[:, BLOCK:], line0[:, :BLOCK]], axis=1))
    line1 = jnp.where(lax.rem(b1, 2) == 1, line1, jnp.concatenate([line1[:, BLOCK:], line1[:, :BLOCK]], axis=1))
    label_row = jnp.where(first_half, line0, line1)
    label_col = jnp.sum(jnp.where(diagonal, label_row, 0), axis=1, keepdims=True)

    def count_lower(r, count):
        return count + jnp.where(seg_ref[pl.ds(r, 1), :] < label_col, 1, 0)

    count = lax.fori_loop(0, nc, count_lower, jnp.zeros((SPAN, SPAN), jnp.int32))
    start_col = jnp.sum(count, axis=1, keepdims=True)
    start_row = jnp.sum(jnp.where(diagonal, start_col, 0), axis=0, keepdims=True)
    swapped = jnp.concatenate([start_row[:, BLOCK:], start_row[:, :BLOCK]], axis=1)
    shape4 = (PIECES, SEEN, 8, SPAN)
    key_place = (
        lax.broadcasted_iota(jnp.int32, shape4, 0) * 8
        + lax.broadcasted_iota(jnp.int32, shape4, 1) * BLOCK
        + lax.broadcasted_iota(jnp.int32, shape4, 2)
    ).reshape(WINDOW, SPAN)
    high = BACK * BLOCK + jnp.where(first_half, lane[:1], lane[:1] - BLOCK)
    for i, b in enumerate((b0, b1)):
        both = jnp.where(first_half, start_row, swapped) if i == 0 else jnp.where(first_half, swapped, start_row)
        low = both - (b - BACK) * BLOCK
        bias[i] = jnp.where((key_place >= low) & (key_place <= high), 0.0, NEVER)

    for i in range(2):
        for head in range(GROUP):
            part = do_ref[i * BLOCK : (i + 1) * BLOCK, head * SPAN : (head + 1) * SPAN].astype(f32)
            dot_t[i, :, head * BLOCK : (head + 1) * BLOCK] = part.T

    await_bytes(r1.at[pl.ds(0, nc - 1)], recv_sem.at[1])
    stored[...] = r1[...].astype(f32).reshape(blocks, 8, SPAN)
    seq[pl.ds(0, BACK)] = jnp.zeros((BACK, 8, SPAN), f32)

    def to_sequence(b, _):
        seq[b + BACK] = stored[place[0, b]]
        return 0

    lax.fori_loop(0, blocks, to_sequence, 0, unroll=8)

    def windows_of(j):
        both = [seq[pl.ds(order[0, 2 * j + i], SEEN)] for i in range(2)]
        return jnp.concatenate(both, axis=0).reshape(2 * PART, SPAN).astype(bf16)

    def send_windows(e, _):
        j = member(c, e)
        s2[e] = windows_of(j)
        remote(s2.at[e], r2.at[rank_of(c)], 3, {"ctx": j}).start()
        return 0

    lax.fori_loop(1, CLASSES, send_windows, 0)
    r2[rank_of(c)] = windows_of(c)
    await_bytes(r2.at[pl.ds(0, CLASSES - 1)], recv_sem.at[3])
    for kind, target in enumerate((keys, vals)):
        for i in range(2):
            for piece in range(PIECES):
                both = r2[kind * PIECES + piece].astype(f32)
                target[i, piece * PART : (piece + 1) * PART, :] = both[i * PART : (i + 1) * PART]
    if nh > 1:
        await_bytes(q_loc.at[pl.ds(0, (nh - 1) * rows), :], recv_sem.at[2])

    scale = SPAN ** (-0.5)
    power = scale * float(np.log2(np.e))
    key_grads, value_grads = [], []
    for i in range(2):
        key_tile, value_tile = keys[i].astype(bf16), vals[i].astype(bf16)
        block = pl.ds(i * BLOCK, BLOCK)
        for part in range(GROUP * BLOCK // LANES):
            heads = range(part * LANES // BLOCK, (part + 1) * LANES // BLOCK)
            lanes = slice(part * LANES, (part + 1) * LANES)
            query = jnp.concatenate([q_loc[block, a * SPAN : (a + 1) * SPAN] for a in heads], axis=0)
            cotangent = jnp.concatenate([do_ref[block, a * SPAN : (a + 1) * SPAN] for a in heads], axis=0)
            scores = lax.dot_general(key_tile, query, NT, preferred_element_type=f32)
            scores = scores + jnp.concatenate([bias[i]] * (LANES // SPAN), axis=1)
            top = jnp.max(scores, axis=0, keepdims=True)
            raised = jnp.exp2((scores - top) * power)
            total = jnp.sum(raised, axis=0, keepdims=True)
            sums = lax.dot_general(value_tile, raised.astype(bf16), TN, preferred_element_type=f32)
            inverse = 1.0 / total
            attended = (sums * inverse).astype(bf16).astype(f32)
            dsum = jnp.sum(dot_t[i, :, lanes] * attended, axis=0, keepdims=True)
            prob = raised * inverse
            probs[:, lanes] = prob.astype(bf16)
            dprob = lax.dot_general(value_tile, cotangent, NT, preferred_element_type=f32)
            dscore = (prob * (dprob - dsum)).astype(bf16)
            dscores[:, lanes] = dscore
            query_grad = lax.dot_general(key_tile, dscore, TN, preferred_element_type=f32) * scale
            attended_rows = attended.T.astype(bf16)
            query_grad_rows = query_grad.T.astype(bf16)
            for n, a in enumerate(heads):
                att_out[block, a * SPAN : (a + 1) * SPAN] = attended_rows[n * BLOCK : (n + 1) * BLOCK]
                dq_loc[block, a * SPAN : (a + 1) * SPAN] = query_grad_rows[n * BLOCK : (n + 1) * BLOCK]
        query = jnp.concatenate([q_loc[block, a * SPAN : (a + 1) * SPAN] for a in range(GROUP)], axis=0)
        cotangent = jnp.concatenate([do_ref[block, a * SPAN : (a + 1) * SPAN] for a in range(GROUP)], axis=0)
        keys[i] = jnp.dot(dscores[...], query, preferred_element_type=f32) * scale
        vals[i] = jnp.dot(probs[...], cotangent, preferred_element_type=f32)

    for kind, source in enumerate((keys, vals)):
        for piece in range(PIECES):
            both = [source[i, piece * PART : (piece + 1) * PART, :] for i in range(2)]
            s3[kind * PIECES + piece] = jnp.concatenate(both, axis=0).astype(bf16)

    def send_back(e, _):
        j = member(c, e)
        remote(s3.at[rank_of(j)], r3.at[rank_of(c)], 4, {"ctx": j}).start()
        return 0

    lax.fori_loop(1, CLASSES, send_back, 0)
    r3[rank_of(c)] = s3[rank_of(c)]

    await_bytes(r3.at[pl.ds(0, CLASSES - 1)], recv_sem.at[4])
    r3f[pl.ds(0, 2 * CLASSES)] = r3[...].astype(f32).reshape(2 * CLASSES, SEEN, 8, SPAN)
    r3f[2 * CLASSES] = jnp.zeros((SEEN, 8, SPAN), f32)

    def add_up(b, sums):
        s = place[0, b]
        j = s // 2
        slot = jnp.where(j // CLASSES == c // CLASSES, rank_of(j) * 2 + lax.rem(s, 2), 2 * CLASSES)
        new = r3f[slot]
        sums = [sums[k] + new[k] for k in range(SEEN)]
        acc[b] = sums[0]
        return tuple(sums[1:]) + (jnp.zeros((8, SPAN), f32),)

    sums = lax.fori_loop(0, blocks, add_up, tuple(jnp.zeros((8, SPAN), f32) for _ in range(SEEN)), unroll=4)
    for k in range(BACK):
        acc[blocks + k] = sums[k]

    def tile_of(j):
        both = [acc[order[0, 2 * j + i] + BACK] for i in range(2)]
        return jnp.concatenate(both, axis=0).astype(bf16)

    def send_sums(d, _):
        j = lax.rem(c + d, nc)
        s4[j] = tile_of(j)
        remote(s4.at[j], r4.at[c], 6, {"ctx": j}).start()
        return 0

    lax.fori_loop(1, nc, send_sums, 0)
    r4[c] = tile_of(c)

    def send_dq(d, _):
        g = lax.rem(h + d, nh)
        remote(dq_loc.at[own_rows(g), :], dq_out.at[:, head_columns(h, wide)], 5, {"head": g}).start()
        return 0

    lax.fori_loop(1, nh, send_dq, 0)
    dq_out[:, head_columns(h, wide)] = dq_loc[own_rows(h), :]

    await_bytes(r4.at[pl.ds(0, nc - 1)], recv_sem.at[6])
    for kind in range(2):
        uppers, lowers = [], []
        for piece in range(PIECES):
            base = (piece // LINE) * LINE * PAIR + kind * LINE + piece % LINE
            tile = r4[base].astype(f32)
            for copy in range(1, nc // CLASSES):
                tile = tile + r4[copy * CLASSES + base].astype(f32)
            uppers.append(tile[:8])
            lowers.append(tile[8:])
        dkv_loc[kind] = jnp.concatenate(uppers + lowers, axis=0).astype(bf16)

    def send_dkv(d, _):
        g = lax.rem(h + d, nh)
        remote(dkv_loc.at[0, own_rows(g), :], dk_out.at[:, head_columns(h, SPAN)], 7, {"head": g}).start()
        remote(dkv_loc.at[1, own_rows(g), :], dv_out.at[:, head_columns(h, SPAN)], 7, {"head": g}).start()
        return 0

    lax.fori_loop(1, nh, send_dkv, 0)
    dk_out[:, head_columns(h, SPAN)] = dkv_loc[0, own_rows(h), :]
    dv_out[:, head_columns(h, SPAN)] = dkv_loc[1, own_rows(h), :]

    some = pl.ds(0, (nh - 1) * rows)
    if nh > 1:
        await_bytes(q_loc.at[some, :], recv_sem.at[5])
        await_bytes(kv_loc.at[:, some, :], recv_sem.at[7])
        await_bytes(kv_loc.at[:, some, :], send_sem.at[0])
        await_bytes(q_loc.at[some, :], send_sem.at[2])
        await_bytes(q_loc.at[some, :], send_sem.at[5])
        await_bytes(kv_loc.at[:, some, :], send_sem.at[7])
    await_bytes(r1.at[pl.ds(0, nc - 1)], send_sem.at[1])
    await_bytes(r2.at[pl.ds(0, CLASSES - 1)], send_sem.at[3])
    await_bytes(r3.at[pl.ds(0, CLASSES - 1)], send_sem.at[4])
    await_bytes(r4.at[pl.ds(0, nc - 1)], send_sem.at[6])


def shards(queries, keys, values, output_gradient, segment_ids, block_order):
    nc, nh = lax.axis_size("ctx"), lax.axis_size("head")
    rows, wide, blocks = queries.shape[0], GROUP * SPAN, 2 * nc
    bf16, f32, i32 = jnp.bfloat16, jnp.float32, jnp.int32
    vmem = pl.BlockSpec(memory_space=pltpu.VMEM)
    anywhere = pl.BlockSpec(memory_space=pl.ANY)
    shapes = (
        jax.ShapeDtypeStruct((2 * BLOCK, wide), bf16),
        jax.ShapeDtypeStruct(queries.shape, bf16),
        jax.ShapeDtypeStruct(keys.shape, bf16),
        jax.ShapeDtypeStruct(values.shape, bf16),
    )
    return pl.pallas_call(
        functools.partial(kernel, nc, nh),
        out_shape=shapes,
        in_specs=[anywhere] * 6,
        out_specs=(vmem, vmem, vmem, vmem),
        scratch_shapes=[
            pltpu.VMEM((2 * BLOCK, wide), bf16),
            pltpu.VMEM((2, 2 * BLOCK, SPAN), bf16),
            pltpu.VMEM((CLASSES, 16, SPAN), bf16),
            pltpu.VMEM((nc, 16, SPAN), bf16),
            pltpu.VMEM((blocks, 8, SPAN), f32),
            pltpu.VMEM((blocks + BACK, 8, SPAN), f32),
            pltpu.VMEM((CLASSES, 2 * PART, SPAN), bf16),
            pltpu.VMEM((CLASSES, 2 * PART, SPAN), bf16),
            pltpu.VMEM((2, WINDOW, SPAN), f32),
            pltpu.VMEM((2, WINDOW, SPAN), f32),
            pltpu.VMEM((2, SPAN, GROUP * BLOCK), f32),
            pltpu.VMEM((2, WINDOW, SPAN), f32),
            pltpu.VMEM((WINDOW, GROUP * BLOCK), bf16),
            pltpu.VMEM((WINDOW, GROUP * BLOCK), bf16),
            pltpu.VMEM((2 * BLOCK, wide), bf16),
            pltpu.VMEM((CLASSES, 2 * PART, SPAN), bf16),
            pltpu.VMEM((CLASSES, 2 * PART, SPAN), bf16),
            pltpu.VMEM((2 * CLASSES + 1, SEEN, 8, SPAN), f32),
            pltpu.VMEM((blocks + BACK, 8, SPAN), f32),
            pltpu.VMEM((nc, 16, SPAN), bf16),
            pltpu.VMEM((nc, 16, SPAN), bf16),
            pltpu.VMEM((2, 2 * BLOCK, SPAN), bf16),
            pltpu.VMEM((2 * BLOCK, wide), bf16),
            pltpu.VMEM((nc, 2 * BLOCK), i32),
            pltpu.VMEM((1, blocks), i32),
            pltpu.VMEM((1, blocks), i32),
            pltpu.SMEM((1, blocks), i32),
            pltpu.SMEM((1, blocks), i32),
            pltpu.SemaphoreType.DMA((8,)),
            pltpu.SemaphoreType.DMA((8,)),
            pltpu.SemaphoreType.DMA((8,)),
        ],
        compiler_params=pltpu.CompilerParams(
            collective_id=0, has_side_effects=True, vmem_limit_bytes=63 * 1024 * 1024
        ),
    )(block_order.reshape(1, blocks), queries, keys, values, output_gradient, segment_ids.reshape(nc, 2 * BLOCK))


def solution(mesh):
    in_specs = (
        P(("ctx", "head"), None),
        P(("ctx", "head"), None),
        P(("ctx", "head"), None),
        P("ctx", "head"),
        P(),
        P(),
    )
    out_specs = (
        P("ctx", "head"),
        P(("ctx", "head"), None),
        P(("ctx", "head"), None),
        P(("ctx", "head"), None),
    )
    return jax.shard_map(shards, mesh=mesh, in_specs=in_specs, out_specs=out_specs, check_vma=False)
```

```python
import functools

import jax
import jax.numpy as jnp
import numpy as np
from jax import lax
from jax.experimental import pallas as pl
from jax.experimental.pallas import tpu as pltpu
from jax.sharding import PartitionSpec as P

SPAN = 128
BLOCK = 64
GROUP = 8
BACK = 8
SEEN = BACK + 1
WINDOW = SEEN * BLOCK
LINE = 4
PAIR = 2
PLANE = LINE * PAIR
HEADS = 8
CLASSES = 16
PIECES = 8
PART = SEEN * 8
LANES = 256
NEVER = -1e30

MESH = pl.DeviceIdType.MESH
NT = (((1,), (1,)), ((), ()))
TN = (((0,), (0,)), ((), ()))


def rank_of(c):
    return lax.rem(c // LINE, PAIR) * PIECES + lax.rem(c, LINE) * 2 + lax.rem(c // PLANE, 2)


def member(c, e):
    x = lax.rem(lax.rem(c, LINE) + lax.rem(e, LINE), LINE)
    z = lax.rem(lax.rem(c // LINE, PAIR) + lax.rem(e // LINE, PAIR), PAIR)
    y = lax.rem(lax.rem(c // PLANE, 2) + e // PLANE, 2)
    return (c // CLASSES) * CLASSES + (y * PAIR + z) * LINE + x


def await_bytes(ref, sem):
    pltpu.make_async_copy(ref, ref, sem).wait()


def kernel(
    nc,
    order_hbm, q_ref, k_ref, v_ref, do_hbm, seg_hbm,
    att_out, dq_out, dk_out, dv_out,
    q_loc, dealt, spread, r1, stored, seq, s2, r2, keys, vals, dot_t, bias,
    probs, dscores, dq_loc, s3, r3, r3f, acc, s4, r4, summed,
    do_ref, seg_ref, order_row, place_row, order, place,
    send_sem, recv_sem, local_sem,
):
    c = lax.axis_index("ctx")
    h = lax.axis_index("head")
    y, z, x, zx = c // PLANE, lax.rem(c // LINE, PAIR), lax.rem(c, LINE), lax.rem(c, PLANE)
    ny = nc // PLANE
    rows = q_ref.shape[0]
    wide = GROUP * SPAN
    blocks = 2 * nc
    f32, bf16 = jnp.float32, jnp.bfloat16
    own_deal = x == lax.rem(h, LINE)

    def remote(src, dst, which, where):
        return pltpu.make_async_remote_copy(
            src_ref=src, dst_ref=dst, send_sem=send_sem.at[which], recv_sem=recv_sem.at[which],
            device_id=where, device_id_type=MESH,
        )

    def for_each(low, high, what):
        def step(d, _):
            what(d)
            return 0

        lax.fori_loop(low, high, step, 0)

    barrier = pltpu.get_barrier_semaphore()

    def greet(where):
        pl.semaphore_signal(barrier, inc=1, device_id=where, device_id_type=MESH)

    def greet_dealer(d):
        greet({"ctx": y * PLANE + lax.rem(zx + d // 2, PLANE), "head": x + LINE * lax.rem(d, 2)})

    for_each(2, 2 * PLANE, greet_dealer)
    for half in range(2):

        @pl.when(x + LINE * half != h)
        def _():
            greet({"ctx": c, "head": x + LINE * half})

    for_each(1, CLASSES, lambda e: greet({"ctx": member(c, e)}))
    for_each(1, ny, lambda d: greet({"ctx": lax.rem(c + d * PLANE, nc)}))
    for_each(1, HEADS, lambda d: greet({"head": lax.rem(h + d, HEADS)}))

    def own_rows(g):
        return pl.ds(pl.multiple_of(g * rows, rows), rows)

    def head_columns(g, width):
        return pl.ds(pl.multiple_of(g * width, width), width)

    fetch_order = [
        pltpu.make_async_copy(order_hbm, order, local_sem.at[2]),
        pltpu.make_async_copy(order_hbm, order_row, local_sem.at[3]),
    ]
    fetch_rest = [
        pltpu.make_async_copy(seg_hbm, seg_ref, local_sem.at[4]),
        pltpu.make_async_copy(do_hbm, do_ref, local_sem.at[5]),
        pltpu.make_async_copy(q_ref.at[:, head_columns(h, wide)], q_loc.at[own_rows(h), :], local_sem.at[6]),
    ]
    for fetch in fetch_order + fetch_rest:
        fetch.start()
    for fetch in fetch_order:
        fetch.wait()

    spot = lax.broadcasted_iota(jnp.int32, (blocks, blocks), 0)
    across = lax.broadcasted_iota(jnp.int32, (blocks, blocks), 1)
    order_col = jnp.sum(jnp.where(spot == across, order_row[...], 0), axis=1, keepdims=True)
    place_row[...] = jnp.max(jnp.where(order_col == across, spot, 0), axis=0, keepdims=True)
    fetch_place = pltpu.make_async_copy(place_row, place, local_sem.at[7])
    fetch_place.start()

    others = 2 * PLANE + CLASSES - 1 + ny - 1 + HEADS - 1

    @pl.when(own_deal)
    def _():
        pl.semaphore_wait(barrier, others - 1)

    @pl.when(jnp.logical_not(own_deal))
    def _():
        pl.semaphore_wait(barrier, others)

    slot = zx * 2 + h // LINE
    for kind, source in enumerate((k_ref, v_ref)):
        there = (y * PAIR + kind) * LINE + lax.rem(h, LINE)

        def deal(d):
            g = lax.rem(h + d, HEADS)
            remote(source.at[:, head_columns(g, SPAN)], dealt.at[slot], 0, {"ctx": there, "head": g}).start()

        for_each(1, HEADS, deal)
        stays = own_deal & (z == kind)

        @pl.when(jnp.logical_not(stays))
        def _():
            deal(0)

        @pl.when(stays)
        def _():
            pltpu.make_async_copy(source.at[:, head_columns(h, SPAN)], dealt.at[slot], recv_sem.at[0]).start()

    await_bytes(dealt, recv_sem.at[0])

    halves = dealt[...].astype(f32).reshape(PLANE, 2, 2, 8, SPAN)
    for half in range(2):
        spread[half] = halves[:, :, half].reshape(PLANE, 16, SPAN).astype(bf16)

    def own_plane(there):
        return pl.ds(there * PLANE, PLANE)

    def send_spread(d):
        there = lax.rem(y + d, ny)
        remote(spread.at[lax.rem(there, 2)], r1.at[own_plane(y)], 1, {"ctx": there * PLANE + zx}).start()

    for_each(1, ny, send_spread)
    r1[own_plane(y)] = spread[lax.rem(y, 2)]

    def send_q(d):
        g = lax.rem(h + d, HEADS)
        remote(q_ref.at[:, head_columns(g, wide)], q_loc.at[own_rows(h), :], 2, {"head": g}).start()

    for_each(1, HEADS, send_q)
    for fetch in fetch_rest:
        fetch.wait()
    fetch_place.wait()

    lane = lax.broadcasted_iota(jnp.int32, (SPAN, SPAN), 1)
    diagonal = lane == lax.broadcasted_iota(jnp.int32, (SPAN, SPAN), 0)
    first_half = lane[:1] < BLOCK
    b0, b1 = order[0, 2 * c], order[0, 2 * c + 1]
    line0 = seg_ref[pl.ds(b0 // 2, 1), :]
    line1 = seg_ref[pl.ds(b1 // 2, 1), :]
    line0 = jnp.where(lax.rem(b0, 2) == 0, line0, jnp.concatenate([line0[:, BLOCK:], line0[:, :BLOCK]], axis=1))
    line1 = jnp.where(lax.rem(b1, 2) == 1, line1, jnp.concatenate([line1[:, BLOCK:], line1[:, :BLOCK]], axis=1))
    label_row = jnp.where(first_half, line0, line1)
    label_col = jnp.sum(jnp.where(diagonal, label_row, 0), axis=1, keepdims=True)

    def count_lower(r, count):
        return count + jnp.where(seg_ref[pl.ds(r, 1), :] < label_col, 1, 0)

    count = lax.fori_loop(0, nc, count_lower, jnp.zeros((SPAN, SPAN), jnp.int32))
    start_col = jnp.sum(count, axis=1, keepdims=True)
    start_row = jnp.sum(jnp.where(diagonal, start_col, 0), axis=0, keepdims=True)
    swapped = jnp.concatenate([start_row[:, BLOCK:], start_row[:, :BLOCK]], axis=1)
    shape4 = (PIECES, SEEN, 8, SPAN)
    key_place = (
        lax.broadcasted_iota(jnp.int32, shape4, 0) * 8
        + lax.broadcasted_iota(jnp.int32, shape4, 1) * BLOCK
        + lax.broadcasted_iota(jnp.int32, shape4, 2)
    ).reshape(WINDOW, SPAN)
    high = BACK * BLOCK + jnp.where(first_half, lane[:1], lane[:1] - BLOCK)
    for i, b in enumerate((b0, b1)):
        both = jnp.where(first_half, start_row, swapped) if i == 0 else jnp.where(first_half, swapped, start_row)
        low = both - (b - BACK) * BLOCK
        bias[i] = jnp.where((key_place >= low) & (key_place <= high), 0.0, NEVER)

    for i in range(2):
        for head in range(GROUP):
            part = do_ref[i * BLOCK : (i + 1) * BLOCK, head * SPAN : (head + 1) * SPAN].astype(f32)
            dot_t[i, :, head * BLOCK : (head + 1) * BLOCK] = part.T

    await_bytes(r1.at[pl.ds(0, (ny - 1) * PLANE)], recv_sem.at[1])
    stored[...] = r1[...].astype(f32).reshape(blocks, 8, SPAN)
    seq[pl.ds(0, BACK)] = jnp.zeros((BACK, 8, SPAN), f32)

    def to_sequence(b, _):
        seq[b + BACK] = stored[place[0, b]]
        return 0

    lax.fori_loop(0, blocks, to_sequence, 0, unroll=8)
    first, second = pl.ds(0, PART + 8), pl.ds(PART + 8, PART - 8)

    def first_of(j):
        both = [seq[pl.ds(order[0, 2 * j], SEEN)], seq[pl.ds(order[0, 2 * j + 1], 1)]]
        return jnp.concatenate(both, axis=0).reshape(PART + 8, SPAN).astype(bf16)

    def second_of(j):
        return seq[pl.ds(order[0, 2 * j + 1] + 1, SEEN - 1)].reshape(PART - 8, SPAN).astype(bf16)

    def send_first(e):
        j = member(c, e)
        s2[e, first, :] = first_of(j)
        remote(s2.at[e, first, :], r2.at[rank_of(c), first, :], 3, {"ctx": j}).start()

    def send_second(e):
        j = member(c, e)
        s2[e, second, :] = second_of(j)
        remote(s2.at[e, second, :], r2.at[rank_of(c), second, :], 8, {"ctx": j}).start()

    for_each(1, CLASSES, send_first)
    for_each(1, CLASSES, send_second)
    r2[rank_of(c), first, :] = first_of(c)
    r2[rank_of(c), second, :] = second_of(c)
    peers = pl.ds(0, CLASSES - 1)
    some = pl.ds(0, (HEADS - 1) * rows)

    early, late = pl.ds(0, PART - 8), pl.ds(PART - 8, PART + 8)
    scale = SPAN ** (-0.5)
    power = scale * float(np.log2(np.e))
    for i in range(2):
        await_bytes(r2.at[peers, (first, second)[i], :], recv_sem.at[(3, 8)[i]])
        for kind, target in enumerate((keys, vals)):
            for piece in range(PIECES):
                near = r2[kind * PIECES + piece, i * (PART - 8) : i * (PART - 8) + PART + 8, :].astype(f32)
                target[i, piece * PART : (piece + 1) * PART, :] = near[8 * i : 8 * i + PART]
        if i == 0:
            await_bytes(q_loc.at[some, :], recv_sem.at[2])
        key_tile, value_tile = keys[i].astype(bf16), vals[i].astype(bf16)
        block = pl.ds(i * BLOCK, BLOCK)
        for part in range(GROUP * BLOCK // LANES):
            heads = range(part * LANES // BLOCK, (part + 1) * LANES // BLOCK)
            lanes = slice(part * LANES, (part + 1) * LANES)
            query = jnp.concatenate([q_loc[block, a * SPAN : (a + 1) * SPAN] for a in heads], axis=0)
            cotangent = jnp.concatenate([do_ref[block, a * SPAN : (a + 1) * SPAN] for a in heads], axis=0)
            scores = lax.dot_general(key_tile, query, NT, preferred_element_type=f32)
            scores = scores + jnp.concatenate([bias[i]] * (LANES // SPAN), axis=1)
            top = jnp.max(scores, axis=0, keepdims=True)
            raised = jnp.exp2((scores - top) * power)
            total = jnp.sum(raised, axis=0, keepdims=True)
            sums = lax.dot_general(value_tile, raised.astype(bf16), TN, preferred_element_type=f32)
            inverse = 1.0 / total
            attended = (sums * inverse).astype(bf16).astype(f32)
            dsum = jnp.sum(dot_t[i, :, lanes] * attended, axis=0, keepdims=True)
            prob = raised * inverse
            probs[:, lanes] = prob.astype(bf16)
            dprob = lax.dot_general(value_tile, cotangent, NT, preferred_element_type=f32)
            dscore = (prob * (dprob - dsum)).astype(bf16)
            dscores[:, lanes] = dscore
            query_grad = lax.dot_general(key_tile, dscore, TN, preferred_element_type=f32) * scale
            attended_rows = attended.T.astype(bf16)
            query_grad_rows = query_grad.T.astype(bf16)
            for n, a in enumerate(heads):
                att_out[block, a * SPAN : (a + 1) * SPAN] = attended_rows[n * BLOCK : (n + 1) * BLOCK]
                dq_loc[block, a * SPAN : (a + 1) * SPAN] = query_grad_rows[n * BLOCK : (n + 1) * BLOCK]
        query = jnp.concatenate([q_loc[block, a * SPAN : (a + 1) * SPAN] for a in range(GROUP)], axis=0)
        cotangent = jnp.concatenate([do_ref[block, a * SPAN : (a + 1) * SPAN] for a in range(GROUP)], axis=0)
        keys[i] = jnp.dot(dscores[...], query, preferred_element_type=f32) * scale
        vals[i] = jnp.dot(probs[...], cotangent, preferred_element_type=f32)


        part, which = ((early, 4), (late, 9))[i]
        for kind, source in enumerate((keys, vals)):
            for piece in range(PIECES):
                mine = source[i, piece * PART : (piece + 1) * PART, :]
                if i == 0:
                    s3[kind * PIECES + piece, early, :] = mine[: PART - 8].astype(bf16)
                else:
                    before = source[0, piece * PART + PART - 8 : (piece + 1) * PART, :]
                    s3[kind * PIECES + piece, late, :] = jnp.concatenate([before, mine], axis=0).astype(bf16)

        def send_back(e):
            j = member(c, e)
            remote(s3.at[rank_of(j), part, :], r3.at[rank_of(c), part, :], which, {"ctx": j}).start()

        for_each(1, CLASSES, send_back)
        r3[rank_of(c), part, :] = s3[rank_of(c), part, :]

    await_bytes(r3.at[peers, early, :], recv_sem.at[4])
    await_bytes(r3.at[peers, late, :], recv_sem.at[9])
    r3f[pl.ds(0, 2 * CLASSES)] = r3[...].astype(f32).reshape(2 * CLASSES, SEEN, 8, SPAN)
    r3f[2 * CLASSES] = jnp.zeros((SEEN, 8, SPAN), f32)

    def add_up(b, sums):
        s = place[0, b]
        j = s // 2
        slot = jnp.where(j // CLASSES == c // CLASSES, rank_of(j) * 2 + lax.rem(s, 2), 2 * CLASSES)
        new = r3f[slot]
        sums = [sums[k] + new[k] for k in range(SEEN)]
        acc[b] = sums[0]
        return tuple(sums[1:]) + (jnp.zeros((8, SPAN), f32),)

    sums = lax.fori_loop(0, blocks, add_up, tuple(jnp.zeros((8, SPAN), f32) for _ in range(SEEN)), unroll=4)
    for k in range(BACK):
        acc[blocks + k] = sums[k]

    def tiles_of(there):
        tiles = []
        for n in range(PLANE):
            both = [acc[order[0, 2 * (there * PLANE + n) + i] + BACK] for i in range(2)]
            tiles.append(jnp.concatenate(both, axis=0).astype(bf16))
        return jnp.stack(tiles)

    def send_sums(d):
        there = lax.rem(y + d, ny)
        s4[there] = tiles_of(there)
        remote(s4.at[there], r4.at[y], 6, {"ctx": there * PLANE + zx}).start()

    for_each(1, ny, send_sums)
    r4[y] = tiles_of(y)

    def send_dq(d):
        g = lax.rem(h + d, HEADS)
        remote(dq_loc.at[own_rows(g), :], dq_out.at[:, head_columns(h, wide)], 5, {"head": g}).start()

    for_each(1, HEADS, send_dq)
    dq_out[:, head_columns(h, wide)] = dq_loc[own_rows(h), :]

    await_bytes(r4.at[pl.ds(0, ny - 1)], recv_sem.at[6])
    parts = []
    for half in range(2):
        part = r4[half].astype(f32)
        for there in range(half + 2, ny, 2):
            part = part + r4[there].astype(f32)
        parts.append(part.reshape(2 * PLANE, 8, SPAN))
    summed[...] = jnp.concatenate(parts, axis=1).astype(bf16)

    for kind, out in enumerate((dk_out, dv_out)):

        def send_sum(d):
            n, half = lax.rem(zx + d // 2, PLANE), lax.rem(d, 2)
            remote(
                summed.at[2 * n + half], out.at[:, head_columns(h, SPAN)], 7,
                {"ctx": y * PLANE + n, "head": half * LINE + x},
            ).start()

        @pl.when(z == kind)
        def _():
            for_each(2, 2 * PLANE, send_sum)
            for half in range(2):

                @pl.when(half * LINE + x != h)
                def _():
                    send_sum(half)

                @pl.when(half * LINE + x == h)
                def _():
                    pltpu.make_async_copy(
                        summed.at[2 * zx + half], out.at[:, head_columns(h, SPAN)], recv_sem.at[7]
                    ).start()

    await_bytes(q_loc.at[some, :], recv_sem.at[5])
    await_bytes(dealt, recv_sem.at[7])
    await_bytes(r1.at[pl.ds(0, (ny - 1) * PLANE)], send_sem.at[1])
    await_bytes(q_loc.at[some, :], send_sem.at[2])
    await_bytes(r2.at[peers, first, :], send_sem.at[3])
    await_bytes(r2.at[peers, second, :], send_sem.at[8])
    await_bytes(r3.at[peers, early, :], send_sem.at[4])
    await_bytes(r3.at[peers, late, :], send_sem.at[9])
    await_bytes(q_loc.at[some, :], send_sem.at[5])
    await_bytes(r4.at[pl.ds(0, ny - 1)], send_sem.at[6])
    for which in (0, 7):

        @pl.when(own_deal)
        def _():
            await_bytes(dealt.at[pl.ds(0, 2 * PLANE - 1)], send_sem.at[which])

        @pl.when(jnp.logical_not(own_deal))
        def _():
            await_bytes(dealt, send_sem.at[which])


def shards(queries, keys, values, output_gradient, segment_ids, block_order):
    nc = lax.axis_size("ctx")
    wide, blocks = GROUP * SPAN, 2 * nc
    bf16, f32, i32 = jnp.bfloat16, jnp.float32, jnp.int32
    vmem = pl.BlockSpec(memory_space=pltpu.VMEM)
    anywhere = pl.BlockSpec(memory_space=pl.ANY)
    shapes = (
        jax.ShapeDtypeStruct((2 * BLOCK, wide), bf16),
        jax.ShapeDtypeStruct(queries.shape, bf16),
        jax.ShapeDtypeStruct(keys.shape, bf16),
        jax.ShapeDtypeStruct(values.shape, bf16),
    )
    return pl.pallas_call(
        functools.partial(kernel, nc),
        out_shape=shapes,
        in_specs=[anywhere] * 6,
        out_specs=(vmem, vmem, vmem, vmem),
        scratch_shapes=[
            pltpu.VMEM((2 * BLOCK, wide), bf16),
            pltpu.VMEM((2 * PLANE, 16, SPAN), bf16),
            pltpu.VMEM((2, PLANE, 16, SPAN), bf16),
            pltpu.VMEM((nc, 16, SPAN), bf16),
            pltpu.VMEM((blocks, 8, SPAN), f32),
            pltpu.VMEM((blocks + BACK, 8, SPAN), f32),
            pltpu.VMEM((CLASSES, 2 * PART, SPAN), bf16),
            pltpu.VMEM((CLASSES, 2 * PART, SPAN), bf16),
            pltpu.VMEM((2, WINDOW, SPAN), f32),
            pltpu.VMEM((2, WINDOW, SPAN), f32),
            pltpu.VMEM((2, SPAN, GROUP * BLOCK), f32),
            pltpu.VMEM((2, WINDOW, SPAN), f32),
            pltpu.VMEM((WINDOW, GROUP * BLOCK), bf16),
            pltpu.VMEM((WINDOW, GROUP * BLOCK), bf16),
            pltpu.VMEM((2 * BLOCK, wide), bf16),
            pltpu.VMEM((CLASSES, 2 * PART, SPAN), bf16),
            pltpu.VMEM((CLASSES, 2 * PART, SPAN), bf16),
            pltpu.VMEM((2 * CLASSES + 1, SEEN, 8, SPAN), f32),
            pltpu.VMEM((blocks + BACK, 8, SPAN), f32),
            pltpu.VMEM((nc // PLANE, PLANE, 16, SPAN), bf16),
            pltpu.VMEM((nc // PLANE, PLANE, 16, SPAN), bf16),
            pltpu.VMEM((2 * PLANE, 16, SPAN), bf16),
            pltpu.VMEM((2 * BLOCK, wide), bf16),
            pltpu.VMEM((nc, 2 * BLOCK), i32),
            pltpu.VMEM((1, blocks), i32),
            pltpu.VMEM((1, blocks), i32),
            pltpu.SMEM((1, blocks), i32),
            pltpu.SMEM((1, blocks), i32),
            pltpu.SemaphoreType.DMA((10,)),
            pltpu.SemaphoreType.DMA((10,)),
            pltpu.SemaphoreType.DMA((8,)),
        ],
        compiler_params=pltpu.CompilerParams(
            collective_id=0, has_side_effects=True, vmem_limit_bytes=63 * 1024 * 1024
        ),
    )(block_order.reshape(1, blocks), queries, keys, values, output_gradient, segment_ids.reshape(nc, 2 * BLOCK))


def solution(mesh):
    in_specs = (
        P(("ctx", "head"), None),
        P(("ctx", "head"), None),
        P(("ctx", "head"), None),
        P("ctx", "head"),
        P(),
        P(),
    )
    out_specs = (
        P("ctx", "head"),
        P(("ctx", "head"), None),
        P(("ctx", "head"), None),
        P(("ctx", "head"), None),
    )
    return jax.shard_map(shards, mesh=mesh, in_specs=in_specs, out_specs=out_specs, check_vma=False)
```

```python
import functools

import jax
import jax.numpy as jnp
import numpy as np
from jax import lax
from jax.experimental import pallas as pl
from jax.experimental.pallas import tpu as pltpu
from jax.sharding import PartitionSpec as P

SPAN = 128
BLOCK = 64
GROUP = 8
BACK = 8
SEEN = BACK + 1
WINDOW = SEEN * BLOCK
LINE = 4
PAIR = 2
PLANE = LINE * PAIR
HEADS = 8
CLASSES = 16
PIECES = 8
PART = SEEN * 8
LANES = 256
NEVER = -1e30

MESH = pl.DeviceIdType.MESH
NT = (((1,), (1,)), ((), ()))
TN = (((0,), (0,)), ((), ()))


def rank_of(c):
    return lax.rem(c // LINE, PAIR) * PIECES + lax.rem(c, LINE) * 2 + lax.rem(c // PLANE, 2)


def member(c, e):
    x = lax.rem(lax.rem(c, LINE) + lax.rem(e, LINE), LINE)
    z = lax.rem(lax.rem(c // LINE, PAIR) + lax.rem(e // LINE, PAIR), PAIR)
    y = lax.rem(lax.rem(c // PLANE, 2) + e // PLANE, 2)
    return (c // CLASSES) * CLASSES + (y * PAIR + z) * LINE + x


def await_bytes(ref, sem):
    pltpu.make_async_copy(ref, ref, sem).wait()


def kernel(
    nc,
    order_hbm, q_ref, k_ref, v_ref, do_hbm, seg_hbm,
    att_out, dq_out, dk_out, dv_out,
    q_loc, dealt, spread, r1, stored, seq, s2, r2, keys, vals, dot_t, bias,
    probs, dscores, dq_loc, s3, r3, r3f, acc, s4, r4, summed,
    do_ref, seg_ref, order_row, place_row, order, place,
    send_sem, recv_sem, local_sem,
):
    c = lax.axis_index("ctx")
    h = lax.axis_index("head")
    y, z, x, zx = c // PLANE, lax.rem(c // LINE, PAIR), lax.rem(c, LINE), lax.rem(c, PLANE)
    ny = nc // PLANE
    rows = q_ref.shape[0]
    wide = GROUP * SPAN
    blocks = 2 * nc
    f32, bf16 = jnp.float32, jnp.bfloat16
    own_deal = x == lax.rem(h, LINE)

    def remote(src, dst, which, where):
        return pltpu.make_async_remote_copy(
            src_ref=src, dst_ref=dst, send_sem=send_sem.at[which], recv_sem=recv_sem.at[which],
            device_id=where, device_id_type=MESH,
        )

    def far_first(k):
        return 4 + (k // 2) * (1 - 2 * lax.rem(k, 2))

    def for_each(low, high, what):
        def step(d, _):
            what(d)
            return 0

        lax.fori_loop(low, high, step, 0)

    def far_plane(k):
        return ny // 2 + (k // 2) * (1 - 2 * lax.rem(k, 2))

    barrier = pltpu.get_barrier_semaphore()

    def greet(where):
        pl.semaphore_signal(barrier, inc=1, device_id=where, device_id_type=MESH)

    def greet_dealer(d):
        greet({"ctx": y * PLANE + lax.rem(zx + d // 2, PLANE), "head": x + LINE * lax.rem(d, 2)})

    for_each(2, 2 * PLANE, lambda k: greet_dealer(2 * PLANE + 1 - k))
    for half in range(2):

        @pl.when(x + LINE * half != h)
        def _():
            greet({"ctx": c, "head": x + LINE * half})

    for_each(1, ny, lambda k: greet({"ctx": lax.rem(c + far_plane(k) * PLANE, nc)}))
    for_each(1, HEADS, lambda k: greet({"head": lax.rem(h + far_first(k), HEADS)}))
    for_each(1, CLASSES, lambda k: greet({"ctx": member(c, CLASSES - k)}))

    def own_rows(g):
        return pl.ds(pl.multiple_of(g * rows, rows), rows)

    def head_columns(g, width):
        return pl.ds(pl.multiple_of(g * width, width), width)

    fetch_order = [
        pltpu.make_async_copy(order_hbm, order, local_sem.at[2]),
        pltpu.make_async_copy(order_hbm, order_row, local_sem.at[3]),
    ]
    fetch_rest = [
        pltpu.make_async_copy(seg_hbm, seg_ref, local_sem.at[4]),
        pltpu.make_async_copy(do_hbm, do_ref, local_sem.at[5]),
        pltpu.make_async_copy(q_ref.at[:, head_columns(h, wide)], q_loc.at[own_rows(h), :], local_sem.at[6]),
    ]
    for fetch in fetch_order + fetch_rest:
        fetch.start()
    for fetch in fetch_order:
        fetch.wait()

    spot = lax.broadcasted_iota(jnp.int32, (blocks, blocks), 0)
    across = lax.broadcasted_iota(jnp.int32, (blocks, blocks), 1)
    order_col = jnp.sum(jnp.where(spot == across, order_row[...], 0), axis=1, keepdims=True)
    place_row[...] = jnp.max(jnp.where(order_col == across, spot, 0), axis=0, keepdims=True)
    fetch_place = pltpu.make_async_copy(place_row, place, local_sem.at[7])
    fetch_place.start()

    others = 2 * PLANE + CLASSES - 1 + ny - 1 + HEADS - 1

    @pl.when(own_deal)
    def _():
        pl.semaphore_wait(barrier, others - 1)

    @pl.when(jnp.logical_not(own_deal))
    def _():
        pl.semaphore_wait(barrier, others)

    slot = zx * 2 + h // LINE
    for kind, source in enumerate((k_ref, v_ref)):
        there = (y * PAIR + kind) * LINE + lax.rem(h, LINE)

        def deal(d):
            g = lax.rem(h + d, HEADS)
            remote(source.at[:, head_columns(g, SPAN)], dealt.at[slot], 0, {"ctx": there, "head": g}).start()

        for_each(1, HEADS, lambda k: deal(far_first(k)))
        stays = own_deal & (z == kind)

        @pl.when(jnp.logical_not(stays))
        def _():
            deal(0)

        @pl.when(stays)
        def _():
            pltpu.make_async_copy(source.at[:, head_columns(h, SPAN)], dealt.at[slot], recv_sem.at[0]).start()

    await_bytes(dealt, recv_sem.at[0])

    halves = dealt[...].astype(f32).reshape(PLANE, 2, 2, 8, SPAN)
    for half in range(2):
        spread[half] = halves[:, :, half].reshape(PLANE, 16, SPAN).astype(bf16)

    def own_plane(there):
        return pl.ds(there * PLANE, PLANE)

    def send_spread(d):
        there = lax.rem(y + d, ny)
        remote(spread.at[lax.rem(there, 2)], r1.at[own_plane(y)], 1, {"ctx": there * PLANE + zx}).start()

    for_each(1, ny, lambda k: send_spread(far_plane(k)))
    r1[own_plane(y)] = spread[lax.rem(y, 2)]

    def send_q(d):
        g = lax.rem(h + d, HEADS)
        remote(q_ref.at[:, head_columns(g, wide)], q_loc.at[own_rows(h), :], 2, {"head": g}).start()

    for_each(1, HEADS, lambda k: send_q(far_first(k)))
    for fetch in fetch_rest:
        fetch.wait()
    fetch_place.wait()

    lane = lax.broadcasted_iota(jnp.int32, (SPAN, SPAN), 1)
    diagonal = lane == lax.broadcasted_iota(jnp.int32, (SPAN, SPAN), 0)
    first_half = lane[:1] < BLOCK
    b0, b1 = order[0, 2 * c], order[0, 2 * c + 1]
    line0 = seg_ref[pl.ds(b0 // 2, 1), :]
    line1 = seg_ref[pl.ds(b1 // 2, 1), :]
    line0 = jnp.where(lax.rem(b0, 2) == 0, line0, jnp.concatenate([line0[:, BLOCK:], line0[:, :BLOCK]], axis=1))
    line1 = jnp.where(lax.rem(b1, 2) == 1, line1, jnp.concatenate([line1[:, BLOCK:], line1[:, :BLOCK]], axis=1))
    label_row = jnp.where(first_half, line0, line1)
    label_col = jnp.sum(jnp.where(diagonal, label_row, 0), axis=1, keepdims=True)

    def count_lower(r, count):
        return count + jnp.where(seg_ref[pl.ds(r, 1), :] < label_col, 1, 0)

    count = lax.fori_loop(0, nc, count_lower, jnp.zeros((SPAN, SPAN), jnp.int32))
    start_col = jnp.sum(count, axis=1, keepdims=True)
    start_row = jnp.sum(jnp.where(diagonal, start_col, 0), axis=0, keepdims=True)
    swapped = jnp.concatenate([start_row[:, BLOCK:], start_row[:, :BLOCK]], axis=1)
    shape4 = (PIECES, SEEN, 8, SPAN)
    key_place = (
        lax.broadcasted_iota(jnp.int32, shape4, 0) * 8
        + lax.broadcasted_iota(jnp.int32, shape4, 1) * BLOCK
        + lax.broadcasted_iota(jnp.int32, shape4, 2)
    ).reshape(WINDOW, SPAN)
    high = BACK * BLOCK + jnp.where(first_half, lane[:1], lane[:1] - BLOCK)
    for i, b in enumerate((b0, b1)):
        both = jnp.where(first_half, start_row, swapped) if i == 0 else jnp.where(first_half, swapped, start_row)
        low = both - (b - BACK) * BLOCK
        bias[i] = jnp.where((key_place >= low) & (key_place <= high), 0.0, NEVER)

    for i in range(2):
        for head in range(GROUP):
            part = do_ref[i * BLOCK : (i + 1) * BLOCK, head * SPAN : (head + 1) * SPAN].astype(f32)
            dot_t[i, :, head * BLOCK : (head + 1) * BLOCK] = part.T

    await_bytes(r1.at[pl.ds(0, (ny - 1) * PLANE)], recv_sem.at[1])
    stored[...] = r1[...].astype(f32).reshape(blocks, 8, SPAN)
    seq[pl.ds(0, BACK)] = jnp.zeros((BACK, 8, SPAN), f32)

    def to_sequence(b, _):
        seq[b + BACK] = stored[place[0, b]]
        return 0

    lax.fori_loop(0, blocks, to_sequence, 0, unroll=8)
    first, second = pl.ds(0, PART + 8), pl.ds(PART + 8, PART - 8)

    def first_of(j):
        both = [seq[pl.ds(order[0, 2 * j], SEEN)], seq[pl.ds(order[0, 2 * j + 1], 1)]]
        return jnp.concatenate(both, axis=0).reshape(PART + 8, SPAN).astype(bf16)

    def second_of(j):
        return seq[pl.ds(order[0, 2 * j + 1] + 1, SEEN - 1)].reshape(PART - 8, SPAN).astype(bf16)

    def send_first(e):
        j = member(c, e)
        s2[e, first, :] = first_of(j)
        remote(s2.at[e, first, :], r2.at[rank_of(c), first, :], 3, {"ctx": j}).start()

    def send_second(e):
        j = member(c, e)
        s2[e, second, :] = second_of(j)
        remote(s2.at[e, second, :], r2.at[rank_of(c), second, :], 8, {"ctx": j}).start()

    for_each(1, CLASSES, lambda k: send_first(CLASSES - k))
    for_each(1, CLASSES, lambda k: send_second(CLASSES - k))
    r2[rank_of(c), first, :] = first_of(c)
    r2[rank_of(c), second, :] = second_of(c)
    peers = pl.ds(0, CLASSES - 1)
    some = pl.ds(0, (HEADS - 1) * rows)

    early, late = pl.ds(0, PART - 8), pl.ds(PART - 8, PART + 8)
    scale = SPAN ** (-0.5)
    power = scale * float(np.log2(np.e))
    for i in range(2):
        await_bytes(r2.at[peers, (first, second)[i], :], recv_sem.at[(3, 8)[i]])
        for kind, target in enumerate((keys, vals)):
            for piece in range(PIECES):
                near = r2[kind * PIECES + piece, i * (PART - 8) : i * (PART - 8) + PART + 8, :].astype(f32)
                target[i, piece * PART : (piece + 1) * PART, :] = near[8 * i : 8 * i + PART]
        if i == 0:
            await_bytes(q_loc.at[some, :], recv_sem.at[2])
        key_tile, value_tile = keys[i].astype(bf16), vals[i].astype(bf16)
        block = pl.ds(i * BLOCK, BLOCK)
        for part in range(GROUP * BLOCK // LANES):
            heads = range(part * LANES // BLOCK, (part + 1) * LANES // BLOCK)
            lanes = slice(part * LANES, (part + 1) * LANES)
            query = jnp.concatenate([q_loc[block, a * SPAN : (a + 1) * SPAN] for a in heads], axis=0)
            cotangent = jnp.concatenate([do_ref[block, a * SPAN : (a + 1) * SPAN] for a in heads], axis=0)
            scores = lax.dot_general(key_tile, query, NT, preferred_element_type=f32)
            scores = scores + jnp.concatenate([bias[i]] * (LANES // SPAN), axis=1)
            top = jnp.max(scores, axis=0, keepdims=True)
            raised = jnp.exp2((scores - top) * power)
            total = jnp.sum(raised, axis=0, keepdims=True)
            sums = lax.dot_general(value_tile, raised.astype(bf16), TN, preferred_element_type=f32)
            inverse = 1.0 / total
            attended = (sums * inverse).astype(bf16).astype(f32)
            dsum = jnp.sum(dot_t[i, :, lanes] * attended, axis=0, keepdims=True)
            prob = raised * inverse
            probs[:, lanes] = prob.astype(bf16)
            dprob = lax.dot_general(value_tile, cotangent, NT, preferred_element_type=f32)
            dscore = (prob * (dprob - dsum)).astype(bf16)
            dscores[:, lanes] = dscore
            query_grad = lax.dot_general(key_tile, dscore, TN, preferred_element_type=f32) * scale
            attended_rows = attended.T.astype(bf16)
            query_grad_rows = query_grad.T.astype(bf16)
            for n, a in enumerate(heads):
                att_out[block, a * SPAN : (a + 1) * SPAN] = attended_rows[n * BLOCK : (n + 1) * BLOCK]
                dq_loc[block, a * SPAN : (a + 1) * SPAN] = query_grad_rows[n * BLOCK : (n + 1) * BLOCK]
        query = jnp.concatenate([q_loc[block, a * SPAN : (a + 1) * SPAN] for a in range(GROUP)], axis=0)
        cotangent = jnp.concatenate([do_ref[block, a * SPAN : (a + 1) * SPAN] for a in range(GROUP)], axis=0)
        keys[i] = jnp.dot(dscores[...], query, preferred_element_type=f32) * scale
        vals[i] = jnp.dot(probs[...], cotangent, preferred_element_type=f32)


        part, which = ((early, 4), (late, 9))[i]
        for kind, source in enumerate((keys, vals)):
            for piece in range(PIECES):
                mine = source[i, piece * PART : (piece + 1) * PART, :]
                if i == 0:
                    s3[kind * PIECES + piece, early, :] = mine[: PART - 8].astype(bf16)
                else:
                    before = source[0, piece * PART + PART - 8 : (piece + 1) * PART, :]
                    s3[kind * PIECES + piece, late, :] = jnp.concatenate([before, mine], axis=0).astype(bf16)

        def send_back(e):
            j = member(c, e)
            remote(s3.at[rank_of(j), part, :], r3.at[rank_of(c), part, :], which, {"ctx": j}).start()

        for_each(1, CLASSES, lambda k: send_back(CLASSES - k))
        r3[rank_of(c), part, :] = s3[rank_of(c), part, :]

    await_bytes(r3.at[peers, early, :], recv_sem.at[4])
    await_bytes(r3.at[peers, late, :], recv_sem.at[9])
    r3f[pl.ds(0, 2 * CLASSES)] = r3[...].astype(f32).reshape(2 * CLASSES, SEEN, 8, SPAN)
    r3f[2 * CLASSES] = jnp.zeros((SEEN, 8, SPAN), f32)

    def add_up(b, sums):
        s = place[0, b]
        j = s // 2
        slot = jnp.where(j // CLASSES == c // CLASSES, rank_of(j) * 2 + lax.rem(s, 2), 2 * CLASSES)
        new = r3f[slot]
        sums = [sums[k] + new[k] for k in range(SEEN)]
        acc[b] = sums[0]
        return tuple(sums[1:]) + (jnp.zeros((8, SPAN), f32),)

    sums = lax.fori_loop(0, blocks, add_up, tuple(jnp.zeros((8, SPAN), f32) for _ in range(SEEN)), unroll=4)
    for k in range(BACK):
        acc[blocks + k] = sums[k]

    def tiles_of(there):
        tiles = []
        for n in range(PLANE):
            both = [acc[order[0, 2 * (there * PLANE + n) + i] + BACK] for i in range(2)]
            tiles.append(jnp.concatenate(both, axis=0).astype(bf16))
        return jnp.stack(tiles)

    def send_sums(d):
        there = lax.rem(y + d, ny)
        s4[there] = tiles_of(there)
        remote(s4.at[there], r4.at[y], 6, {"ctx": there * PLANE + zx}).start()

    for_each(1, ny, lambda k: send_sums(far_plane(k)))
    r4[y] = tiles_of(y)

    def send_dq(d):
        g = lax.rem(h + d, HEADS)
        remote(dq_loc.at[own_rows(g), :], dq_out.at[:, head_columns(h, wide)], 5, {"head": g}).start()

    for_each(1, HEADS, lambda k: send_dq(far_first(k)))
    dq_out[:, head_columns(h, wide)] = dq_loc[own_rows(h), :]

    await_bytes(r4.at[pl.ds(0, ny - 1)], recv_sem.at[6])
    parts = []
    for half in range(2):
        part = r4[half].astype(f32)
        for there in range(half + 2, ny, 2):
            part = part + r4[there].astype(f32)
        parts.append(part.reshape(2 * PLANE, 8, SPAN))
    summed[...] = jnp.concatenate(parts, axis=1).astype(bf16)

    for kind, out in enumerate((dk_out, dv_out)):

        def send_sum(d):
            n, half = lax.rem(zx + d // 2, PLANE), lax.rem(d, 2)
            remote(
                summed.at[2 * n + half], out.at[:, head_columns(h, SPAN)], 7,
                {"ctx": y * PLANE + n, "head": half * LINE + x},
            ).start()

        @pl.when(z == kind)
        def _():
            for_each(2, 2 * PLANE, send_sum)
            for half in range(2):

                @pl.when(half * LINE + x != h)
                def _():
                    send_sum(half)

                @pl.when(half * LINE + x == h)
                def _():
                    pltpu.make_async_copy(
                        summed.at[2 * zx + half], out.at[:, head_columns(h, SPAN)], recv_sem.at[7]
                    ).start()

    await_bytes(q_loc.at[some, :], recv_sem.at[5])
    await_bytes(dealt, recv_sem.at[7])
    await_bytes(r1.at[pl.ds(0, (ny - 1) * PLANE)], send_sem.at[1])
    await_bytes(q_loc.at[some, :], send_sem.at[2])
    await_bytes(r2.at[peers, first, :], send_sem.at[3])
    await_bytes(r2.at[peers, second, :], send_sem.at[8])
    await_bytes(r3.at[peers, early, :], send_sem.at[4])
    await_bytes(r3.at[peers, late, :], send_sem.at[9])
    await_bytes(q_loc.at[some, :], send_sem.at[5])
    await_bytes(r4.at[pl.ds(0, ny - 1)], send_sem.at[6])
    for which in (0, 7):

        @pl.when(own_deal)
        def _():
            await_bytes(dealt.at[pl.ds(0, 2 * PLANE - 1)], send_sem.at[which])

        @pl.when(jnp.logical_not(own_deal))
        def _():
            await_bytes(dealt, send_sem.at[which])


def shards(queries, keys, values, output_gradient, segment_ids, block_order):
    nc = lax.axis_size("ctx")
    wide, blocks = GROUP * SPAN, 2 * nc
    bf16, f32, i32 = jnp.bfloat16, jnp.float32, jnp.int32
    vmem = pl.BlockSpec(memory_space=pltpu.VMEM)
    anywhere = pl.BlockSpec(memory_space=pl.ANY)
    shapes = (
        jax.ShapeDtypeStruct((2 * BLOCK, wide), bf16),
        jax.ShapeDtypeStruct(queries.shape, bf16),
        jax.ShapeDtypeStruct(keys.shape, bf16),
        jax.ShapeDtypeStruct(values.shape, bf16),
    )
    return pl.pallas_call(
        functools.partial(kernel, nc),
        out_shape=shapes,
        in_specs=[anywhere] * 6,
        out_specs=(vmem, vmem, vmem, vmem),
        scratch_shapes=[
            pltpu.VMEM((2 * BLOCK, wide), bf16),
            pltpu.VMEM((2 * PLANE, 16, SPAN), bf16),
            pltpu.VMEM((2, PLANE, 16, SPAN), bf16),
            pltpu.VMEM((nc, 16, SPAN), bf16),
            pltpu.VMEM((blocks, 8, SPAN), f32),
            pltpu.VMEM((blocks + BACK, 8, SPAN), f32),
            pltpu.VMEM((CLASSES, 2 * PART, SPAN), bf16),
            pltpu.VMEM((CLASSES, 2 * PART, SPAN), bf16),
            pltpu.VMEM((2, WINDOW, SPAN), f32),
            pltpu.VMEM((2, WINDOW, SPAN), f32),
            pltpu.VMEM((2, SPAN, GROUP * BLOCK), f32),
            pltpu.VMEM((2, WINDOW, SPAN), f32),
            pltpu.VMEM((WINDOW, GROUP * BLOCK), bf16),
            pltpu.VMEM((WINDOW, GROUP * BLOCK), bf16),
            pltpu.VMEM((2 * BLOCK, wide), bf16),
            pltpu.VMEM((CLASSES, 2 * PART, SPAN), bf16),
            pltpu.VMEM((CLASSES, 2 * PART, SPAN), bf16),
            pltpu.VMEM((2 * CLASSES + 1, SEEN, 8, SPAN), f32),
            pltpu.VMEM((blocks + BACK, 8, SPAN), f32),
            pltpu.VMEM((nc // PLANE, PLANE, 16, SPAN), bf16),
            pltpu.VMEM((nc // PLANE, PLANE, 16, SPAN), bf16),
            pltpu.VMEM((2 * PLANE, 16, SPAN), bf16),
            pltpu.VMEM((2 * BLOCK, wide), bf16),
            pltpu.VMEM((nc, 2 * BLOCK), i32),
            pltpu.VMEM((1, blocks), i32),
            pltpu.VMEM((1, blocks), i32),
            pltpu.SMEM((1, blocks), i32),
            pltpu.SMEM((1, blocks), i32),
            pltpu.SemaphoreType.DMA((10,)),
            pltpu.SemaphoreType.DMA((10,)),
            pltpu.SemaphoreType.DMA((8,)),
        ],
        compiler_params=pltpu.CompilerParams(
            collective_id=0, has_side_effects=True, vmem_limit_bytes=48 * 1024 * 1024
        ),
    )(*(pltpu.with_memory_space_constraint(a, pltpu.HBM) for a in (block_order.reshape(1, blocks), queries, keys, values, output_gradient, segment_ids.reshape(nc, 2 * BLOCK))))


def solution(mesh):
    in_specs = (
        P(("ctx", "head"), None),
        P(("ctx", "head"), None),
        P(("ctx", "head"), None),
        P("ctx", "head"),
        P(),
        P(),
    )
    out_specs = (
        P("ctx", "head"),
        P(("ctx", "head"), None),
        P(("ctx", "head"), None),
        P(("ctx", "head"), None),
    )
    return jax.shard_map(shards, mesh=mesh, in_specs=in_specs, out_specs=out_specs, check_vma=False)
```

```python
import functools

import jax
import jax.numpy as jnp
import numpy as np
from jax import lax
from jax.experimental import pallas as pl
from jax.experimental.pallas import tpu as pltpu
from jax.sharding import PartitionSpec as P

SPAN = 128
BLOCK = 64
GROUP = 8
BACK = 8
SEEN = BACK + 1
WINDOW = SEEN * BLOCK
LINE = 4
PAIR = 2
PLANE = LINE * PAIR
HEADS = 8
CLASSES = 16
PIECES = 8
PART = SEEN * 8
NEVER = -1e30

MESH = pl.DeviceIdType.MESH
NT = (((1,), (1,)), ((), ()))
TN = (((0,), (0,)), ((), ()))


def rank_of(c):
    return lax.rem(c // LINE, PAIR) * PIECES + lax.rem(c, LINE) * 2 + lax.rem(c // PLANE, 2)


def member(c, e):
    x = lax.rem(lax.rem(c, LINE) + lax.rem(e, LINE), LINE)
    z = lax.rem(lax.rem(c // LINE, PAIR) + lax.rem(e // LINE, PAIR), PAIR)
    y = lax.rem(lax.rem(c // PLANE, 2) + e // PLANE, 2)
    return (c // CLASSES) * CLASSES + (y * PAIR + z) * LINE + x


def await_bytes(ref, sem):
    pltpu.make_async_copy(ref, ref, sem).wait()


def kernel(
    nc,
    order_hbm, q_ref, k_ref, v_ref, do_hbm, seg_hbm,
    att_out, dq_out, dk_out, dv_out,
    q_loc, dealt, spread, r1, stored, seq, s2, r2, keys, vals, dot_t, bias,
    dscores, dq_loc, s3, r3, r3f, acc, s4, r4, summed,
    do_ref, seg_ref, order_row, place_row, order, place, slots,
    send_sem, recv_sem, local_sem,
):
    c = lax.axis_index("ctx")
    h = lax.axis_index("head")
    y, z, x, zx = c // PLANE, lax.rem(c // LINE, PAIR), lax.rem(c, LINE), lax.rem(c, PLANE)
    ny = nc // PLANE
    rows = q_ref.shape[0]
    wide = GROUP * SPAN
    blocks = 2 * nc
    f32, bf16 = jnp.float32, jnp.bfloat16
    own_deal = x == lax.rem(h, LINE)

    def remote(src, dst, which, where):
        return pltpu.make_async_remote_copy(
            src_ref=src, dst_ref=dst, send_sem=send_sem.at[which], recv_sem=recv_sem.at[which],
            device_id=where, device_id_type=MESH,
        )

    def far_first(k):
        return 4 + (k // 2) * (1 - 2 * lax.rem(k, 2))

    def for_each(low, high, what):
        def step(d, _):
            what(d)
            return 0

        lax.fori_loop(low, high, step, 0)

    def far_plane(k):
        return ny // 2 + (k // 2) * (1 - 2 * lax.rem(k, 2))

    barrier = pltpu.get_barrier_semaphore()

    def greet(where):
        pl.semaphore_signal(barrier, inc=1, device_id=where, device_id_type=MESH)

    def greet_dealer(d):
        greet({"ctx": y * PLANE + lax.rem(zx + d // 2, PLANE), "head": x + LINE * lax.rem(d, 2)})

    for_each(2, 2 * PLANE, lambda k: greet_dealer(2 * PLANE + 1 - k))
    for half in range(2):

        @pl.when(x + LINE * half != h)
        def _():
            greet({"ctx": c, "head": x + LINE * half})

    for_each(1, ny, lambda k: greet({"ctx": lax.rem(c + far_plane(k) * PLANE, nc)}))
    for_each(1, HEADS, lambda k: greet({"head": lax.rem(h + far_first(k), HEADS)}))
    for_each(1, CLASSES, lambda k: greet({"ctx": member(c, CLASSES - k)}))

    def own_rows(g):
        return pl.ds(pl.multiple_of(g * rows, rows), rows)

    def head_columns(g, width):
        return pl.ds(pl.multiple_of(g * width, width), width)

    fetch_order = [
        pltpu.make_async_copy(order_hbm, order, local_sem.at[2]),
        pltpu.make_async_copy(order_hbm, order_row, local_sem.at[3]),
    ]
    fetch_rest = [
        pltpu.make_async_copy(seg_hbm, seg_ref, local_sem.at[4]),
        pltpu.make_async_copy(do_hbm, do_ref, local_sem.at[5]),
        pltpu.make_async_copy(q_ref.at[:, head_columns(h, wide)], q_loc.at[own_rows(h), :], local_sem.at[6]),
    ]
    for fetch in fetch_order + fetch_rest:
        fetch.start()
    others = 2 * PLANE + CLASSES - 1 + ny - 1 + HEADS - 1

    @pl.when(own_deal)
    def _():
        pl.semaphore_wait(barrier, others - 1)

    @pl.when(jnp.logical_not(own_deal))
    def _():
        pl.semaphore_wait(barrier, others)

    slot = zx * 2 + h // LINE
    for kind, source in enumerate((k_ref, v_ref)):
        there = (y * PAIR + kind) * LINE + lax.rem(h, LINE)

        def deal(d):
            g = lax.rem(h + d, HEADS)
            remote(source.at[:, head_columns(g, SPAN)], dealt.at[slot], 0, {"ctx": there, "head": g}).start()

        for_each(1, HEADS, lambda k: deal(far_first(k)))
        stays = own_deal & (z == kind)

        @pl.when(jnp.logical_not(stays))
        def _():
            deal(0)

        @pl.when(stays)
        def _():
            pltpu.make_async_copy(source.at[:, head_columns(h, SPAN)], dealt.at[slot], recv_sem.at[0]).start()

    for fetch in fetch_order:
        fetch.wait()

    spot = lax.broadcasted_iota(jnp.int32, (blocks, blocks), 0)
    across = lax.broadcasted_iota(jnp.int32, (blocks, blocks), 1)
    order_col = jnp.sum(jnp.where(spot == across, order_row[...], 0), axis=1, keepdims=True)
    place_row[...] = jnp.max(jnp.where(order_col == across, spot, 0), axis=0, keepdims=True)
    fetch_place = pltpu.make_async_copy(place_row, place, local_sem.at[7])
    fetch_place.start()

    await_bytes(dealt, recv_sem.at[0])

    halves = dealt[...].astype(f32).reshape(PLANE, 2, 2, 8, SPAN)
    for half in range(2):
        spread[half] = halves[:, :, half].reshape(PLANE, 16, SPAN).astype(bf16)

    def own_plane(there):
        return pl.ds(there * PLANE, PLANE)

    def send_spread(d):
        there = lax.rem(y + d, ny)
        remote(spread.at[lax.rem(there, 2)], r1.at[own_plane(y)], 1, {"ctx": there * PLANE + zx}).start()

    for_each(1, ny, lambda k: send_spread(far_plane(k)))
    r1[own_plane(y)] = spread[lax.rem(y, 2)]

    def send_q(d):
        g = lax.rem(h + d, HEADS)
        remote(q_ref.at[:, head_columns(g, wide)], q_loc.at[own_rows(h), :], 2, {"head": g}).start()

    for_each(1, HEADS, lambda k: send_q(far_first(k)))
    for fetch in fetch_rest:
        fetch.wait()
    fetch_place.wait()

    lane = lax.broadcasted_iota(jnp.int32, (SPAN, SPAN), 1)
    diagonal = lane == lax.broadcasted_iota(jnp.int32, (SPAN, SPAN), 0)
    first_half = lane[:1] < BLOCK
    b0, b1 = order[0, 2 * c], order[0, 2 * c + 1]
    line0 = seg_ref[pl.ds(b0 // 2, 1), :]
    line1 = seg_ref[pl.ds(b1 // 2, 1), :]
    line0 = jnp.where(lax.rem(b0, 2) == 0, line0, jnp.concatenate([line0[:, BLOCK:], line0[:, :BLOCK]], axis=1))
    line1 = jnp.where(lax.rem(b1, 2) == 1, line1, jnp.concatenate([line1[:, BLOCK:], line1[:, :BLOCK]], axis=1))
    label_row = jnp.where(first_half, line0, line1)
    label_col = jnp.sum(jnp.where(diagonal, label_row, 0), axis=1, keepdims=True)

    def count_lower(r, count):
        return count + jnp.where(seg_ref[pl.ds(r, 1), :] < label_col, 1, 0)

    count = lax.fori_loop(0, nc, count_lower, jnp.zeros((SPAN, SPAN), jnp.int32))
    start_col = jnp.sum(count, axis=1, keepdims=True)
    start_row = jnp.sum(jnp.where(diagonal, start_col, 0), axis=0, keepdims=True)
    swapped = jnp.concatenate([start_row[:, BLOCK:], start_row[:, :BLOCK]], axis=1)
    shape4 = (PIECES, SEEN, 8, SPAN)
    key_place = (
        lax.broadcasted_iota(jnp.int32, shape4, 0) * 8
        + lax.broadcasted_iota(jnp.int32, shape4, 1) * BLOCK
        + lax.broadcasted_iota(jnp.int32, shape4, 2)
    ).reshape(WINDOW, SPAN)
    high = BACK * BLOCK + jnp.where(first_half, lane[:1], lane[:1] - BLOCK)
    for i, b in enumerate((b0, b1)):
        both = jnp.where(first_half, start_row, swapped) if i == 0 else jnp.where(first_half, swapped, start_row)
        low = both - (b - BACK) * BLOCK
        bias[i] = jnp.where((key_place >= low) & (key_place <= high), 0.0, NEVER)

    def find_slot(b, _):
        s = place[0, b]
        j = s // 2
        slots[0, b] = jnp.where(j // CLASSES == c // CLASSES, rank_of(j) * 2 + lax.rem(s, 2), 2 * CLASSES)
        return 0

    lax.fori_loop(0, blocks, find_slot, 0)

    for i in range(2):
        for head in range(GROUP):
            part = do_ref[i * BLOCK : (i + 1) * BLOCK, head * SPAN : (head + 1) * SPAN].astype(f32)
            dot_t[i, :, head * BLOCK : (head + 1) * BLOCK] = part.T

    await_bytes(r1.at[pl.ds(0, (ny - 1) * PLANE)], recv_sem.at[1])
    stored[...] = r1[...].astype(f32).reshape(blocks, 8, SPAN)
    seq[pl.ds(0, BACK)] = jnp.zeros((BACK, 8, SPAN), f32)

    def to_sequence(b, _):
        seq[b + BACK] = stored[place[0, b]]
        return 0

    lax.fori_loop(0, blocks, to_sequence, 0, unroll=8)
    first, second = pl.ds(0, PART + 8), pl.ds(PART + 8, PART - 8)

    def first_of(j):
        both = [seq[pl.ds(order[0, 2 * j], SEEN)], seq[pl.ds(order[0, 2 * j + 1], 1)]]
        return jnp.concatenate(both, axis=0).reshape(PART + 8, SPAN).astype(bf16)

    def second_of(j):
        return seq[pl.ds(order[0, 2 * j + 1] + 1, SEEN - 1)].reshape(PART - 8, SPAN).astype(bf16)

    def send_first(e):
        j = member(c, e)
        s2[e, first, :] = first_of(j)
        remote(s2.at[e, first, :], r2.at[rank_of(c), first, :], 3, {"ctx": j}).start()

    def send_second(e):
        j = member(c, e)
        s2[e, second, :] = second_of(j)
        remote(s2.at[e, second, :], r2.at[rank_of(c), second, :], 8, {"ctx": j}).start()

    for_each(1, CLASSES, lambda k: send_first(CLASSES - k))
    for_each(1, CLASSES, lambda k: send_second(CLASSES - k))
    r2[rank_of(c), first, :] = first_of(c)
    r2[rank_of(c), second, :] = second_of(c)
    peers = pl.ds(0, CLASSES - 1)
    some = pl.ds(0, (HEADS - 1) * rows)

    early, late = pl.ds(0, PART - 8), pl.ds(PART - 8, PART + 8)
    scale = SPAN ** (-0.5)
    power = scale * float(np.log2(np.e))
    for i in range(2):
        await_bytes(r2.at[peers, (first, second)[i], :], recv_sem.at[(3, 8)[i]])
        for kind, target in enumerate((keys, vals)):
            for piece in range(PIECES):
                near = r2[kind * PIECES + piece, i * (PART - 8) : i * (PART - 8) + PART + 8, :].astype(f32)
                target[i, piece * PART : (piece + 1) * PART, :] = near[8 * i : 8 * i + PART]
        if i == 0:
            await_bytes(q_loc.at[some, :], recv_sem.at[2])
        key_tile, value_tile = keys[i].astype(bf16), vals[i].astype(bf16)
        block = pl.ds(i * BLOCK, BLOCK)
        heads = range(GROUP)
        query = jnp.concatenate([q_loc[block, a * SPAN : (a + 1) * SPAN] for a in heads], axis=0)
        cotangent = jnp.concatenate([do_ref[block, a * SPAN : (a + 1) * SPAN] for a in heads], axis=0)
        scores = lax.dot_general(key_tile, query, NT, preferred_element_type=f32)
        scores = scores + jnp.concatenate([bias[i]] * (GROUP * BLOCK // SPAN), axis=1)
        top = jnp.max(scores, axis=0, keepdims=True)
        raised = jnp.exp2((scores - top) * power)
        total = jnp.sum(raised, axis=0, keepdims=True)
        sums = lax.dot_general(value_tile, raised.astype(bf16), TN, preferred_element_type=f32)
        inverse = 1.0 / total
        attended = (sums * inverse).astype(bf16).astype(f32)
        dsum = jnp.sum(dot_t[i] * attended, axis=0, keepdims=True)
        prob = raised * inverse
        vals[i] = jnp.dot(prob.astype(bf16), cotangent, preferred_element_type=f32)
        dprob = lax.dot_general(value_tile, cotangent, NT, preferred_element_type=f32)
        dscore = (prob * (dprob - dsum)).astype(bf16)
        dscores[...] = dscore
        keys[i] = jnp.dot(dscore, query, preferred_element_type=f32) * scale

        part, which = ((early, 4), (late, 9))[i]
        for kind, source in enumerate((keys, vals)):
            for piece in range(PIECES):
                mine = source[i, piece * PART : (piece + 1) * PART, :]
                if i == 0:
                    s3[kind * PIECES + piece, early, :] = mine[: PART - 8].astype(bf16)
                else:
                    before = source[0, piece * PART + PART - 8 : (piece + 1) * PART, :]
                    s3[kind * PIECES + piece, late, :] = jnp.concatenate([before, mine], axis=0).astype(bf16)

        def send_back(e):
            j = member(c, e)
            remote(s3.at[rank_of(j), part, :], r3.at[rank_of(c), part, :], which, {"ctx": j}).start()

        for_each(1, CLASSES, lambda k: send_back(CLASSES - k))
        r3[rank_of(c), part, :] = s3[rank_of(c), part, :]

        query_grad = lax.dot_general(key_tile, dscores[...], TN, preferred_element_type=f32) * scale
        attended_rows = attended.T.astype(bf16)
        query_grad_rows = query_grad.T.astype(bf16)
        for a in heads:
            att_out[block, a * SPAN : (a + 1) * SPAN] = attended_rows[a * BLOCK : (a + 1) * BLOCK]
            dq_loc[block, a * SPAN : (a + 1) * SPAN] = query_grad_rows[a * BLOCK : (a + 1) * BLOCK]

    await_bytes(r3.at[peers, early, :], recv_sem.at[4])
    await_bytes(r3.at[peers, late, :], recv_sem.at[9])
    r3f[pl.ds(0, 2 * CLASSES)] = r3[...].astype(f32).reshape(2 * CLASSES, SEEN, 8, SPAN)
    r3f[2 * CLASSES] = jnp.zeros((SEEN, 8, SPAN), f32)

    def add_up(b, sums):
        new = r3f[slots[0, b]]
        sums = [sums[k] + new[k] for k in range(SEEN)]
        acc[b] = sums[0]
        return tuple(sums[1:]) + (jnp.zeros((8, SPAN), f32),)

    sums = lax.fori_loop(0, blocks, add_up, tuple(jnp.zeros((8, SPAN), f32) for _ in range(SEEN)), unroll=4)
    for k in range(BACK):
        acc[blocks + k] = sums[k]

    def tiles_of(there):
        tiles = []
        for n in range(PLANE):
            both = [acc[order[0, 2 * (there * PLANE + n) + i] + BACK] for i in range(2)]
            tiles.append(jnp.concatenate(both, axis=0).astype(bf16))
        return jnp.stack(tiles)

    def send_sums(d):
        there = lax.rem(y + d, ny)
        s4[there] = tiles_of(there)
        remote(s4.at[there], r4.at[y], 6, {"ctx": there * PLANE + zx}).start()

    for_each(1, ny, lambda k: send_sums(far_plane(k)))
    r4[y] = tiles_of(y)

    def send_dq(d):
        g = lax.rem(h + d, HEADS)
        remote(dq_loc.at[own_rows(g), :], dq_out.at[:, head_columns(h, wide)], 5, {"head": g}).start()

    for_each(1, HEADS, lambda k: send_dq(far_first(k)))
    dq_out[:, head_columns(h, wide)] = dq_loc[own_rows(h), :]

    await_bytes(r4.at[pl.ds(0, ny - 1)], recv_sem.at[6])
    parts = []
    for half in range(2):
        part = r4[half].astype(f32)
        for there in range(half + 2, ny, 2):
            part = part + r4[there].astype(f32)
        parts.append(part.reshape(2 * PLANE, 8, SPAN))
    summed[...] = jnp.concatenate(parts, axis=1).astype(bf16)

    for kind, out in enumerate((dk_out, dv_out)):

        def send_sum(d):
            n, half = lax.rem(zx + d // 2, PLANE), lax.rem(d, 2)
            remote(
                summed.at[2 * n + half], out.at[:, head_columns(h, SPAN)], 7,
                {"ctx": y * PLANE + n, "head": half * LINE + x},
            ).start()

        @pl.when(z == kind)
        def _():
            for_each(2, 2 * PLANE, send_sum)
            for half in range(2):

                @pl.when(half * LINE + x != h)
                def _():
                    send_sum(half)

                @pl.when(half * LINE + x == h)
                def _():
                    pltpu.make_async_copy(
                        summed.at[2 * zx + half], out.at[:, head_columns(h, SPAN)], recv_sem.at[7]
                    ).start()

    await_bytes(q_loc.at[some, :], recv_sem.at[5])
    await_bytes(dealt, recv_sem.at[7])
    await_bytes(r1.at[pl.ds(0, (ny - 1) * PLANE)], send_sem.at[1])
    await_bytes(q_loc.at[some, :], send_sem.at[2])
    await_bytes(r2.at[peers, first, :], send_sem.at[3])
    await_bytes(r2.at[peers, second, :], send_sem.at[8])
    await_bytes(r3.at[peers, early, :], send_sem.at[4])
    await_bytes(r3.at[peers, late, :], send_sem.at[9])
    await_bytes(q_loc.at[some, :], send_sem.at[5])
    await_bytes(r4.at[pl.ds(0, ny - 1)], send_sem.at[6])
    for which in (0, 7):

        @pl.when(own_deal)
        def _():
            await_bytes(dealt.at[pl.ds(0, 2 * PLANE - 1)], send_sem.at[which])

        @pl.when(jnp.logical_not(own_deal))
        def _():
            await_bytes(dealt, send_sem.at[which])


def put(*refs):
    sems = refs[-1]
    copies = [pltpu.make_async_copy(a, b, sems.at[i]) for i, (a, b) in enumerate(zip(refs[:4], refs[4:8]))]
    for copy in copies:
        copy.start()
    for copy in copies:
        copy.wait()


def shards(queries, keys, values, output_gradient, segment_ids, block_order):
    nc = lax.axis_size("ctx")
    wide, blocks = GROUP * SPAN, 2 * nc
    bf16, f32, i32 = jnp.bfloat16, jnp.float32, jnp.int32
    vmem = pl.BlockSpec(memory_space=pltpu.VMEM)
    anywhere = pl.BlockSpec(memory_space=pl.ANY)
    shapes = (
        jax.ShapeDtypeStruct((2 * BLOCK, wide), bf16),
        jax.ShapeDtypeStruct(queries.shape, bf16),
        jax.ShapeDtypeStruct(keys.shape, bf16),
        jax.ShapeDtypeStruct(values.shape, bf16),
    )
    results = pl.pallas_call(
        functools.partial(kernel, nc),
        out_shape=shapes,
        in_specs=[anywhere] * 6,
        out_specs=(vmem, vmem, vmem, vmem),
        scratch_shapes=[
            pltpu.VMEM((2 * BLOCK, wide), bf16),
            pltpu.VMEM((2 * PLANE, 16, SPAN), bf16),
            pltpu.VMEM((2, PLANE, 16, SPAN), bf16),
            pltpu.VMEM((nc, 16, SPAN), bf16),
            pltpu.VMEM((blocks, 8, SPAN), f32),
            pltpu.VMEM((blocks + BACK, 8, SPAN), f32),
            pltpu.VMEM((CLASSES, 2 * PART, SPAN), bf16),
            pltpu.VMEM((CLASSES, 2 * PART, SPAN), bf16),
            pltpu.VMEM((2, WINDOW, SPAN), f32),
            pltpu.VMEM((2, WINDOW, SPAN), f32),
            pltpu.VMEM((2, SPAN, GROUP * BLOCK), f32),
            pltpu.VMEM((2, WINDOW, SPAN), f32),
            pltpu.VMEM((WINDOW, GROUP * BLOCK), bf16),
            pltpu.VMEM((2 * BLOCK, wide), bf16),
            pltpu.VMEM((CLASSES, 2 * PART, SPAN), bf16),
            pltpu.VMEM((CLASSES, 2 * PART, SPAN), bf16),
            pltpu.VMEM((2 * CLASSES + 1, SEEN, 8, SPAN), f32),
            pltpu.VMEM((blocks + BACK, 8, SPAN), f32),
            pltpu.VMEM((nc // PLANE, PLANE, 16, SPAN), bf16),
            pltpu.VMEM((nc // PLANE, PLANE, 16, SPAN), bf16),
            pltpu.VMEM((2 * PLANE, 16, SPAN), bf16),
            pltpu.VMEM((2 * BLOCK, wide), bf16),
            pltpu.VMEM((nc, 2 * BLOCK), i32),
            pltpu.VMEM((1, blocks), i32),
            pltpu.VMEM((1, blocks), i32),
            pltpu.SMEM((1, blocks), i32),
            pltpu.SMEM((1, blocks), i32),
            pltpu.SMEM((1, blocks), i32),
            pltpu.SemaphoreType.DMA((10,)),
            pltpu.SemaphoreType.DMA((10,)),
            pltpu.SemaphoreType.DMA((8,)),
        ],
        compiler_params=pltpu.CompilerParams(
            collective_id=0, has_side_effects=True, vmem_limit_bytes=48 * 1024 * 1024
        ),
    )(*(pltpu.with_memory_space_constraint(a, pltpu.HBM) for a in (block_order.reshape(1, blocks), queries, keys, values, output_gradient, segment_ids.reshape(nc, 2 * BLOCK))))
    return pl.pallas_call(
        put,
        out_shape=shapes,
        in_specs=[vmem] * 4,
        out_specs=(pl.BlockSpec(memory_space=pltpu.HBM),) * 4,
        scratch_shapes=[pltpu.SemaphoreType.DMA((4,))],
    )(*(pltpu.with_memory_space_constraint(a, pltpu.VMEM) for a in results))


def solution(mesh):
    in_specs = (
        P(("ctx", "head"), None),
        P(("ctx", "head"), None),
        P(("ctx", "head"), None),
        P("ctx", "head"),
        P(),
        P(),
    )
    out_specs = (
        P("ctx", "head"),
        P(("ctx", "head"), None),
        P(("ctx", "head"), None),
        P(("ctx", "head"), None),
    )
    return jax.shard_map(shards, mesh=mesh, in_specs=in_specs, out_specs=out_specs, check_vma=False)
```

```python
import functools

import jax
import jax.numpy as jnp
import numpy as np
from jax import lax
from jax.experimental import pallas as pl
from jax.experimental.pallas import tpu as pltpu
from jax.sharding import PartitionSpec as P

SPAN = 128
BLOCK = 64
GROUP = 8
BACK = 8
SEEN = BACK + 1
WINDOW = SEEN * BLOCK
LINE = 4
PAIR = 2
PLANE = LINE * PAIR
HEADS = 8
CLASSES = 16
PIECES = 8
PART = SEEN * 8
NEVER = -1e30

MESH = pl.DeviceIdType.MESH
NT = (((1,), (1,)), ((), ()))
TN = (((0,), (0,)), ((), ()))


def rank_of(c):
    return lax.rem(c // LINE, PAIR) * PIECES + lax.rem(c, LINE) * 2 + lax.rem(c // PLANE, 2)


def member(c, e):
    x = lax.rem(lax.rem(c, LINE) + lax.rem(e, LINE), LINE)
    z = lax.rem(lax.rem(c // LINE, PAIR) + lax.rem(e // LINE, PAIR), PAIR)
    y = lax.rem(lax.rem(c // PLANE, 2) + e // PLANE, 2)
    return (c // CLASSES) * CLASSES + (y * PAIR + z) * LINE + x


def await_bytes(ref, sem):
    pltpu.make_async_copy(ref, ref, sem).wait()


def kernel(
    nc,
    order_hbm, q_ref, k_ref, v_ref, do_hbm, seg_hbm,
    att_out, dq_out, dk_out, dv_out,
    q_loc, dealt, spread, r1, stored, seq, s2, r2, keys, vals, dot_t, bias,
    dscores, dq_loc, s3, r3, r3f, acc, s4, r4, summed,
    k_near, v_near, do_ref, seg_ref, order_row, place_row, order, place, slots,
    send_sem, recv_sem, local_sem,
):
    c = lax.axis_index("ctx")
    h = lax.axis_index("head")
    y, z, x, zx = c // PLANE, lax.rem(c // LINE, PAIR), lax.rem(c, LINE), lax.rem(c, PLANE)
    ny = nc // PLANE
    rows = q_ref.shape[0]
    wide = GROUP * SPAN
    blocks = 2 * nc
    f32, bf16 = jnp.float32, jnp.bfloat16
    own_deal = x == lax.rem(h, LINE)

    def remote(src, dst, which, where):
        return pltpu.make_async_remote_copy(
            src_ref=src, dst_ref=dst, send_sem=send_sem.at[which], recv_sem=recv_sem.at[which],
            device_id=where, device_id_type=MESH,
        )

    def far_first(k):
        return 4 + (k // 2) * (1 - 2 * lax.rem(k, 2))

    def for_each(low, high, what):
        def step(d, _):
            what(d)
            return 0

        lax.fori_loop(low, high, step, 0)

    def far_plane(k):
        return ny // 2 + (k // 2) * (1 - 2 * lax.rem(k, 2))

    barrier = pltpu.get_barrier_semaphore()

    def greet(where):
        pl.semaphore_signal(barrier, inc=1, device_id=where, device_id_type=MESH)

    def greet_dealer(d):
        greet({"ctx": y * PLANE + lax.rem(zx + d // 2, PLANE), "head": x + LINE * lax.rem(d, 2)})

    fetch_kv = [
        pltpu.make_async_copy(source, near, local_sem.at[kind])
        for kind, (source, near) in enumerate(((k_ref, k_near), (v_ref, v_near)))
    ]
    for fetch in fetch_kv:
        fetch.start()
    for_each(2, 2 * PLANE, lambda k: greet_dealer(2 * PLANE + 1 - k))
    for half in range(2):

        @pl.when(x + LINE * half != h)
        def _():
            greet({"ctx": c, "head": x + LINE * half})

    for_each(1, ny, lambda k: greet({"ctx": lax.rem(c + far_plane(k) * PLANE, nc)}))
    for_each(1, HEADS, lambda k: greet({"head": lax.rem(h + far_first(k), HEADS)}))
    for_each(1, CLASSES, lambda k: greet({"ctx": member(c, CLASSES - k)}))

    def own_rows(g):
        return pl.ds(pl.multiple_of(g * rows, rows), rows)

    def head_columns(g, width):
        return pl.ds(pl.multiple_of(g * width, width), width)

    fetch_order = [
        pltpu.make_async_copy(order_hbm, order, local_sem.at[2]),
        pltpu.make_async_copy(order_hbm, order_row, local_sem.at[3]),
    ]
    fetch_rest = [
        pltpu.make_async_copy(seg_hbm, seg_ref, local_sem.at[4]),
        pltpu.make_async_copy(do_hbm, do_ref, local_sem.at[5]),
        pltpu.make_async_copy(q_ref.at[:, head_columns(h, wide)], q_loc.at[own_rows(h), :], local_sem.at[6]),
    ]
    for fetch in fetch_order + fetch_rest:
        fetch.start()
    for fetch in fetch_kv:
        fetch.wait()
    others = 2 * PLANE + CLASSES - 1 + ny - 1 + HEADS - 1

    @pl.when(own_deal)
    def _():
        pl.semaphore_wait(barrier, others - 1)

    @pl.when(jnp.logical_not(own_deal))
    def _():
        pl.semaphore_wait(barrier, others)

    slot = zx * 2 + h // LINE
    near = (k_near, v_near)

    def deal(kind, d):
        g = lax.rem(h + d, HEADS)
        there = (y * PAIR + kind) * LINE + lax.rem(h, LINE)
        remote(near[kind].at[:, head_columns(g, SPAN)], dealt.at[slot], 0, {"ctx": there, "head": g}).start()

    def deal_both(k):
        deal(0, far_first(k))
        deal(1, far_first(k))

    for_each(1, HEADS, deal_both)
    for kind in range(2):
        stays = own_deal & (z == kind)

        @pl.when(jnp.logical_not(stays))
        def _():
            deal(kind, 0)

        @pl.when(stays)
        def _():
            pltpu.make_async_copy(near[kind].at[:, head_columns(h, SPAN)], dealt.at[slot], recv_sem.at[0]).start()

    for fetch in fetch_order:
        fetch.wait()

    spot = lax.broadcasted_iota(jnp.int32, (blocks, blocks), 0)
    across = lax.broadcasted_iota(jnp.int32, (blocks, blocks), 1)
    order_col = jnp.sum(jnp.where(spot == across, order_row[...], 0), axis=1, keepdims=True)
    place_row[...] = jnp.max(jnp.where(order_col == across, spot, 0), axis=0, keepdims=True)
    fetch_place = pltpu.make_async_copy(place_row, place, local_sem.at[7])
    fetch_place.start()

    await_bytes(dealt, recv_sem.at[0])

    halves = dealt[...].astype(f32).reshape(PLANE, 2, 2, 8, SPAN)
    for half in range(2):
        spread[half] = halves[:, :, half].reshape(PLANE, 16, SPAN).astype(bf16)

    def own_plane(there):
        return pl.ds(there * PLANE, PLANE)

    def send_spread(d):
        there = lax.rem(y + d, ny)
        remote(spread.at[lax.rem(there, 2)], r1.at[own_plane(y)], 1, {"ctx": there * PLANE + zx}).start()

    for_each(1, ny, lambda k: send_spread(far_plane(k)))
    r1[own_plane(y)] = spread[lax.rem(y, 2)]

    def send_q(d):
        g = lax.rem(h + d, HEADS)
        remote(q_ref.at[:, head_columns(g, wide)], q_loc.at[own_rows(h), :], 2, {"head": g}).start()

    for_each(1, HEADS, lambda k: send_q(far_first(k)))
    for fetch in fetch_rest:
        fetch.wait()
    fetch_place.wait()

    lane = lax.broadcasted_iota(jnp.int32, (SPAN, SPAN), 1)
    diagonal = lane == lax.broadcasted_iota(jnp.int32, (SPAN, SPAN), 0)
    first_half = lane[:1] < BLOCK
    b0, b1 = order[0, 2 * c], order[0, 2 * c + 1]
    line0 = seg_ref[pl.ds(b0 // 2, 1), :]
    line1 = seg_ref[pl.ds(b1 // 2, 1), :]
    line0 = jnp.where(lax.rem(b0, 2) == 0, line0, jnp.concatenate([line0[:, BLOCK:], line0[:, :BLOCK]], axis=1))
    line1 = jnp.where(lax.rem(b1, 2) == 1, line1, jnp.concatenate([line1[:, BLOCK:], line1[:, :BLOCK]], axis=1))
    label_row = jnp.where(first_half, line0, line1)
    label_col = jnp.sum(jnp.where(diagonal, label_row, 0), axis=1, keepdims=True)

    def count_lower(r, count):
        return count + jnp.where(seg_ref[pl.ds(r, 1), :] < label_col, 1, 0)

    count = lax.fori_loop(0, nc, count_lower, jnp.zeros((SPAN, SPAN), jnp.int32))
    start_col = jnp.sum(count, axis=1, keepdims=True)
    start_row = jnp.sum(jnp.where(diagonal, start_col, 0), axis=0, keepdims=True)
    swapped = jnp.concatenate([start_row[:, BLOCK:], start_row[:, :BLOCK]], axis=1)
    shape4 = (PIECES, SEEN, 8, SPAN)
    key_place = (
        lax.broadcasted_iota(jnp.int32, shape4, 0) * 8
        + lax.broadcasted_iota(jnp.int32, shape4, 1) * BLOCK
        + lax.broadcasted_iota(jnp.int32, shape4, 2)
    ).reshape(WINDOW, SPAN)
    high = BACK * BLOCK + jnp.where(first_half, lane[:1], lane[:1] - BLOCK)
    for i, b in enumerate((b0, b1)):
        both = jnp.where(first_half, start_row, swapped) if i == 0 else jnp.where(first_half, swapped, start_row)
        low = both - (b - BACK) * BLOCK
        bias[i] = jnp.where((key_place >= low) & (key_place <= high), 0.0, NEVER)

    def find_slot(b, _):
        s = place[0, b]
        j = s // 2
        slots[0, b] = jnp.where(j // CLASSES == c // CLASSES, rank_of(j) * 2 + lax.rem(s, 2), 2 * CLASSES)
        return 0

    lax.fori_loop(0, blocks, find_slot, 0)

    for i in range(2):
        for head in range(GROUP):
            part = do_ref[i * BLOCK : (i + 1) * BLOCK, head * SPAN : (head + 1) * SPAN].astype(f32)
            dot_t[i, :, head * BLOCK : (head + 1) * BLOCK] = part.T

    await_bytes(r1.at[pl.ds(0, (ny - 1) * PLANE)], recv_sem.at[1])
    stored[...] = r1[...].astype(f32).reshape(blocks, 8, SPAN)
    seq[pl.ds(0, BACK)] = jnp.zeros((BACK, 8, SPAN), f32)

    def to_sequence(b, _):
        seq[b + BACK] = stored[place[0, b]]
        return 0

    lax.fori_loop(0, blocks, to_sequence, 0, unroll=8)
    first, second = pl.ds(0, PART + 8), pl.ds(PART + 8, PART - 8)

    def first_of(j):
        both = [seq[pl.ds(order[0, 2 * j], SEEN)], seq[pl.ds(order[0, 2 * j + 1], 1)]]
        return jnp.concatenate(both, axis=0).reshape(PART + 8, SPAN).astype(bf16)

    def second_of(j):
        return seq[pl.ds(order[0, 2 * j + 1] + 1, SEEN - 1)].reshape(PART - 8, SPAN).astype(bf16)

    def send_first(e):
        j = member(c, e)
        s2[e, first, :] = first_of(j)
        remote(s2.at[e, first, :], r2.at[rank_of(c), first, :], 3, {"ctx": j}).start()

    def send_second(e):
        j = member(c, e)
        s2[e, second, :] = second_of(j)
        remote(s2.at[e, second, :], r2.at[rank_of(c), second, :], 8, {"ctx": j}).start()

    for_each(1, CLASSES, lambda k: send_first(CLASSES - k))
    for_each(1, CLASSES, lambda k: send_second(CLASSES - k))
    r2[rank_of(c), first, :] = first_of(c)
    r2[rank_of(c), second, :] = second_of(c)
    peers = pl.ds(0, CLASSES - 1)
    some = pl.ds(0, (HEADS - 1) * rows)

    early, late = pl.ds(0, PART - 8), pl.ds(PART - 8, PART + 8)
    scale = SPAN ** (-0.5)
    power = scale * float(np.log2(np.e))
    for i in range(2):
        await_bytes(r2.at[peers, (first, second)[i], :], recv_sem.at[(3, 8)[i]])
        for kind, target in enumerate((keys, vals)):
            for piece in range(PIECES):
                near = r2[kind * PIECES + piece, i * (PART - 8) : i * (PART - 8) + PART + 8, :].astype(f32)
                target[i, piece * PART : (piece + 1) * PART, :] = near[8 * i : 8 * i + PART]
        if i == 0:
            await_bytes(q_loc.at[some, :], recv_sem.at[2])
        key_tile, value_tile = keys[i].astype(bf16), vals[i].astype(bf16)
        block = pl.ds(i * BLOCK, BLOCK)
        heads = range(GROUP)
        query = jnp.concatenate([q_loc[block, a * SPAN : (a + 1) * SPAN] for a in heads], axis=0)
        cotangent = jnp.concatenate([do_ref[block, a * SPAN : (a + 1) * SPAN] for a in heads], axis=0)
        scores = lax.dot_general(key_tile, query, NT, preferred_element_type=f32)
        scores = scores + jnp.concatenate([bias[i]] * (GROUP * BLOCK // SPAN), axis=1)
        top = jnp.max(scores, axis=0, keepdims=True)
        raised = jnp.exp2((scores - top) * power)
        total = jnp.sum(raised, axis=0, keepdims=True)
        sums = lax.dot_general(value_tile, raised.astype(bf16), TN, preferred_element_type=f32)
        inverse = 1.0 / total
        attended = (sums * inverse).astype(bf16).astype(f32)
        dsum = jnp.sum(dot_t[i] * attended, axis=0, keepdims=True)
        prob = raised * inverse
        vals[i] = jnp.dot(prob.astype(bf16), cotangent, preferred_element_type=f32)
        dprob = lax.dot_general(value_tile, cotangent, NT, preferred_element_type=f32)
        dscore = (prob * (dprob - dsum)).astype(bf16)
        dscores[...] = dscore
        keys[i] = jnp.dot(dscore, query, preferred_element_type=f32) * scale

        part, which = ((early, 4), (late, 9))[i]
        for kind, source in enumerate((keys, vals)):
            for piece in range(PIECES):
                mine = source[i, piece * PART : (piece + 1) * PART, :]
                if i == 0:
                    s3[kind * PIECES + piece, early, :] = mine[: PART - 8].astype(bf16)
                else:
                    before = source[0, piece * PART + PART - 8 : (piece + 1) * PART, :]
                    s3[kind * PIECES + piece, late, :] = jnp.concatenate([before, mine], axis=0).astype(bf16)

        def send_back(e):
            j = member(c, e)
            remote(s3.at[rank_of(j), part, :], r3.at[rank_of(c), part, :], which, {"ctx": j}).start()

        for_each(1, CLASSES, lambda k: send_back(CLASSES - k))
        r3[rank_of(c), part, :] = s3[rank_of(c), part, :]

        query_grad = lax.dot_general(key_tile, dscores[...], TN, preferred_element_type=f32) * scale
        attended_rows = attended.T.astype(bf16)
        query_grad_rows = query_grad.T.astype(bf16)
        for a in heads:
            att_out[block, a * SPAN : (a + 1) * SPAN] = attended_rows[a * BLOCK : (a + 1) * BLOCK]
            dq_loc[block, a * SPAN : (a + 1) * SPAN] = query_grad_rows[a * BLOCK : (a + 1) * BLOCK]

    await_bytes(r3.at[peers, early, :], recv_sem.at[4])
    await_bytes(r3.at[peers, late, :], recv_sem.at[9])
    r3f[pl.ds(0, 2 * CLASSES)] = r3[...].astype(f32).reshape(2 * CLASSES, SEEN, 8, SPAN)
    r3f[2 * CLASSES] = jnp.zeros((SEEN, 8, SPAN), f32)

    def add_up(b, sums):
        new = r3f[slots[0, b]]
        sums = [sums[k] + new[k] for k in range(SEEN)]
        acc[b] = sums[0]
        return tuple(sums[1:]) + (jnp.zeros((8, SPAN), f32),)

    sums = lax.fori_loop(0, blocks, add_up, tuple(jnp.zeros((8, SPAN), f32) for _ in range(SEEN)), unroll=4)
    for k in range(BACK):
        acc[blocks + k] = sums[k]

    def tiles_of(there):
        tiles = []
        for n in range(PLANE):
            both = [acc[order[0, 2 * (there * PLANE + n) + i] + BACK] for i in range(2)]
            tiles.append(jnp.concatenate(both, axis=0).astype(bf16))
        return jnp.stack(tiles)

    def send_sums(d):
        there = lax.rem(y + d, ny)
        s4[there] = tiles_of(there)
        remote(s4.at[there], r4.at[y], 6, {"ctx": there * PLANE + zx}).start()

    for_each(1, ny, lambda k: send_sums(far_plane(k)))
    r4[y] = tiles_of(y)

    def send_dq(d):
        g = lax.rem(h + d, HEADS)
        remote(dq_loc.at[own_rows(g), :], dq_out.at[:, head_columns(h, wide)], 5, {"head": g}).start()

    for_each(1, HEADS, lambda k: send_dq(far_first(k)))
    dq_out[:, head_columns(h, wide)] = dq_loc[own_rows(h), :]

    await_bytes(r4.at[pl.ds(0, ny - 1)], recv_sem.at[6])
    parts = []
    for half in range(2):
        part = r4[half].astype(f32)
        for there in range(half + 2, ny, 2):
            part = part + r4[there].astype(f32)
        parts.append(part.reshape(2 * PLANE, 8, SPAN))
    summed[...] = jnp.concatenate(parts, axis=1).astype(bf16)

    for kind, out in enumerate((dk_out, dv_out)):

        def send_sum(d):
            n, half = lax.rem(zx + d // 2, PLANE), lax.rem(d, 2)
            remote(
                summed.at[2 * n + half], out.at[:, head_columns(h, SPAN)], 7,
                {"ctx": y * PLANE + n, "head": half * LINE + x},
            ).start()

        @pl.when(z == kind)
        def _():
            for_each(0, 12, lambda k: send_sum(2 * (2 + k // 4 - 3 * (k // 8)) + 8 * lax.rem(k // 2, 2) + lax.rem(k, 2)))
            for_each(8, 10, send_sum)
            for half in range(2):

                @pl.when(half * LINE + x != h)
                def _():
                    send_sum(half)

                @pl.when(half * LINE + x == h)
                def _():
                    pltpu.make_async_copy(
                        summed.at[2 * zx + half], out.at[:, head_columns(h, SPAN)], recv_sem.at[7]
                    ).start()

    await_bytes(q_loc.at[some, :], recv_sem.at[5])
    await_bytes(dealt, recv_sem.at[7])
    await_bytes(r1.at[pl.ds(0, (ny - 1) * PLANE)], send_sem.at[1])
    await_bytes(q_loc.at[some, :], send_sem.at[2])
    await_bytes(r2.at[peers, first, :], send_sem.at[3])
    await_bytes(r2.at[peers, second, :], send_sem.at[8])
    await_bytes(r3.at[peers, early, :], send_sem.at[4])
    await_bytes(r3.at[peers, late, :], send_sem.at[9])
    await_bytes(q_loc.at[some, :], send_sem.at[5])
    await_bytes(r4.at[pl.ds(0, ny - 1)], send_sem.at[6])
    for which in (0, 7):

        @pl.when(own_deal)
        def _():
            await_bytes(dealt.at[pl.ds(0, 2 * PLANE - 1)], send_sem.at[which])

        @pl.when(jnp.logical_not(own_deal))
        def _():
            await_bytes(dealt, send_sem.at[which])


def put(*refs):
    sems = refs[-1]
    copies = [pltpu.make_async_copy(a, b, sems.at[i]) for i, (a, b) in enumerate(zip(refs[:4], refs[4:8]))]
    for copy in copies:
        copy.start()
    for copy in copies:
        copy.wait()


def shards(queries, keys, values, output_gradient, segment_ids, block_order):
    nc = lax.axis_size("ctx")
    wide, blocks = GROUP * SPAN, 2 * nc
    bf16, f32, i32 = jnp.bfloat16, jnp.float32, jnp.int32
    vmem = pl.BlockSpec(memory_space=pltpu.VMEM)
    anywhere = pl.BlockSpec(memory_space=pl.ANY)
    shapes = (
        jax.ShapeDtypeStruct((2 * BLOCK, wide), bf16),
        jax.ShapeDtypeStruct(queries.shape, bf16),
        jax.ShapeDtypeStruct(keys.shape, bf16),
        jax.ShapeDtypeStruct(values.shape, bf16),
    )
    results = pl.pallas_call(
        functools.partial(kernel, nc),
        out_shape=shapes,
        in_specs=[anywhere] * 6,
        out_specs=(vmem, vmem, vmem, vmem),
        scratch_shapes=[
            pltpu.VMEM((2 * BLOCK, wide), bf16),
            pltpu.VMEM((2 * PLANE, 16, SPAN), bf16),
            pltpu.VMEM((2, PLANE, 16, SPAN), bf16),
            pltpu.VMEM((nc, 16, SPAN), bf16),
            pltpu.VMEM((blocks, 8, SPAN), f32),
            pltpu.VMEM((blocks + BACK, 8, SPAN), f32),
            pltpu.VMEM((CLASSES, 2 * PART, SPAN), bf16),
            pltpu.VMEM((CLASSES, 2 * PART, SPAN), bf16),
            pltpu.VMEM((2, WINDOW, SPAN), f32),
            pltpu.VMEM((2, WINDOW, SPAN), f32),
            pltpu.VMEM((2, SPAN, GROUP * BLOCK), f32),
            pltpu.VMEM((2, WINDOW, SPAN), f32),
            pltpu.VMEM((WINDOW, GROUP * BLOCK), bf16),
            pltpu.VMEM((2 * BLOCK, wide), bf16),
            pltpu.VMEM((CLASSES, 2 * PART, SPAN), bf16),
            pltpu.VMEM((CLASSES, 2 * PART, SPAN), bf16),
            pltpu.VMEM((2 * CLASSES + 1, SEEN, 8, SPAN), f32),
            pltpu.VMEM((blocks + BACK, 8, SPAN), f32),
            pltpu.VMEM((nc // PLANE, PLANE, 16, SPAN), bf16),
            pltpu.VMEM((nc // PLANE, PLANE, 16, SPAN), bf16),
            pltpu.VMEM((2 * PLANE, 16, SPAN), bf16),
            pltpu.VMEM(keys.shape, bf16),
            pltpu.VMEM(values.shape, bf16),
            pltpu.VMEM((2 * BLOCK, wide), bf16),
            pltpu.VMEM((nc, 2 * BLOCK), i32),
            pltpu.VMEM((1, blocks), i32),
            pltpu.VMEM((1, blocks), i32),
            pltpu.SMEM((1, blocks), i32),
            pltpu.SMEM((1, blocks), i32),
            pltpu.SMEM((1, blocks), i32),
            pltpu.SemaphoreType.DMA((10,)),
            pltpu.SemaphoreType.DMA((10,)),
            pltpu.SemaphoreType.DMA((8,)),
        ],
        compiler_params=pltpu.CompilerParams(
            collective_id=0, has_side_effects=True, vmem_limit_bytes=48 * 1024 * 1024
        ),
    )(*(pltpu.with_memory_space_constraint(a, pltpu.HBM) for a in (block_order.reshape(1, blocks), queries, keys, values, output_gradient, segment_ids.reshape(nc, 2 * BLOCK))))
    return pl.pallas_call(
        put,
        out_shape=shapes,
        in_specs=[vmem] * 4,
        out_specs=(pl.BlockSpec(memory_space=pltpu.HBM),) * 4,
        scratch_shapes=[pltpu.SemaphoreType.DMA((4,))],
    )(*(pltpu.with_memory_space_constraint(a, pltpu.VMEM) for a in results))


def solution(mesh):
    in_specs = (
        P(("ctx", "head"), None),
        P(("ctx", "head"), None),
        P(("ctx", "head"), None),
        P("ctx", "head"),
        P(),
        P(),
    )
    out_specs = (
        P("ctx", "head"),
        P(("ctx", "head"), None),
        P(("ctx", "head"), None),
        P(("ctx", "head"), None),
    )
    return jax.shard_map(shards, mesh=mesh, in_specs=in_specs, out_specs=out_specs, check_vma=False)
```

```python
import functools

import jax
import jax.numpy as jnp
import numpy as np
from jax import lax
from jax.experimental import pallas as pl
from jax.experimental.pallas import tpu as pltpu
from jax.sharding import PartitionSpec as P

SPAN = 128
BLOCK = 64
GROUP = 8
BACK = 8
SEEN = BACK + 1
WINDOW = SEEN * BLOCK
LINE = 4
PAIR = 2
PLANE = LINE * PAIR
HEADS = 8
CLASSES = 16
PIECES = 8
PART = SEEN * 8
NEVER = -1e30

MESH = pl.DeviceIdType.MESH
NT = (((1,), (1,)), ((), ()))
TN = (((0,), (0,)), ((), ()))


def rank_of(c):
    return lax.rem(c // LINE, PAIR) * PIECES + lax.rem(c, LINE) * 2 + lax.rem(c // PLANE, 2)


def member(c, e):
    x = lax.rem(lax.rem(c, LINE) + lax.rem(e, LINE), LINE)
    z = lax.rem(lax.rem(c // LINE, PAIR) + lax.rem(e // LINE, PAIR), PAIR)
    y = lax.rem(lax.rem(c // PLANE, 2) + e // PLANE, 2)
    return (c // CLASSES) * CLASSES + (y * PAIR + z) * LINE + x


def await_bytes(ref, sem):
    pltpu.make_async_copy(ref, ref, sem).wait()


def kernel(
    nc,
    order_hbm, q_ref, k_ref, v_ref, do_hbm, seg_hbm,
    att_out, dq_out, dk_out, dv_out,
    q_loc, dealt, spread, r1, stored, seq, s2, r2, keys, vals, dot_t, bias,
    dscores, dq_loc, s3, r3, r3f, acc, s4, r4, summed,
    k_near, v_near, do_ref, seg_ref, order_row, place_row, order, place, slots,
    send_sem, recv_sem, local_sem,
):
    c = lax.axis_index("ctx")
    h = lax.axis_index("head")
    y, z, x, zx = c // PLANE, lax.rem(c // LINE, PAIR), lax.rem(c, LINE), lax.rem(c, PLANE)
    ny = nc // PLANE
    rows = q_ref.shape[0]
    wide = GROUP * SPAN
    blocks = 2 * nc
    f32, bf16 = jnp.float32, jnp.bfloat16
    own_deal = x == lax.rem(h, LINE)

    def remote(src, dst, which, where):
        return pltpu.make_async_remote_copy(
            src_ref=src, dst_ref=dst, send_sem=send_sem.at[which], recv_sem=recv_sem.at[which],
            device_id=where, device_id_type=MESH,
        )

    def far_first(k):
        return 4 + (k // 2) * (1 - 2 * lax.rem(k, 2))

    def for_each(low, high, what):
        def step(d, _):
            what(d)
            return 0

        lax.fori_loop(low, high, step, 0, unroll=True)

    def far_plane(k):
        return ny // 2 + (k // 2) * (1 - 2 * lax.rem(k, 2))

    barrier = pltpu.get_barrier_semaphore()

    def greet(where):
        pl.semaphore_signal(barrier, inc=1, device_id=where, device_id_type=MESH)

    def greet_dealer(d):
        greet({"ctx": y * PLANE + lax.rem(zx + d // 2, PLANE), "head": x + LINE * lax.rem(d, 2)})

    fetch_kv = [
        pltpu.make_async_copy(source, near, local_sem.at[kind])
        for kind, (source, near) in enumerate(((k_ref, k_near), (v_ref, v_near)))
    ]
    for fetch in fetch_kv:
        fetch.start()
    for_each(2, 2 * PLANE, lambda k: greet_dealer(2 * PLANE + 1 - k))
    for half in range(2):

        @pl.when(x + LINE * half != h)
        def _():
            greet({"ctx": c, "head": x + LINE * half})

    for_each(1, ny, lambda k: greet({"ctx": lax.rem(c + far_plane(k) * PLANE, nc)}))
    for_each(1, HEADS, lambda k: greet({"head": lax.rem(h + far_first(k), HEADS)}))
    for_each(1, CLASSES, lambda k: greet({"ctx": member(c, CLASSES - k)}))

    def own_rows(g):
        return pl.ds(pl.multiple_of(g * rows, rows), rows)

    def head_columns(g, width):
        return pl.ds(pl.multiple_of(g * width, width), width)

    fetch_order = [
        pltpu.make_async_copy(order_hbm, order, local_sem.at[2]),
        pltpu.make_async_copy(order_hbm, order_row, local_sem.at[3]),
    ]
    fetch_rest = [
        pltpu.make_async_copy(seg_hbm, seg_ref, local_sem.at[4]),
        pltpu.make_async_copy(do_hbm, do_ref, local_sem.at[5]),
        pltpu.make_async_copy(q_ref.at[:, head_columns(h, wide)], q_loc.at[own_rows(h), :], local_sem.at[6]),
    ]
    for fetch in fetch_order + fetch_rest:
        fetch.start()
    for fetch in fetch_kv:
        fetch.wait()
    others = 2 * PLANE + CLASSES - 1 + ny - 1 + HEADS - 1

    @pl.when(own_deal)
    def _():
        pl.semaphore_wait(barrier, others - 1)

    @pl.when(jnp.logical_not(own_deal))
    def _():
        pl.semaphore_wait(barrier, others)

    slot = zx * 2 + h // LINE
    near = (k_near, v_near)

    def deal(kind, d):
        g = lax.rem(h + d, HEADS)
        there = (y * PAIR + kind) * LINE + lax.rem(h, LINE)
        remote(near[kind].at[:, head_columns(g, SPAN)], dealt.at[slot], 0, {"ctx": there, "head": g}).start()

    def deal_both(k):
        deal(0, far_first(k))
        deal(1, far_first(k))

    for_each(1, HEADS, deal_both)
    for kind in range(2):
        stays = own_deal & (z == kind)

        @pl.when(jnp.logical_not(stays))
        def _():
            deal(kind, 0)

        @pl.when(stays)
        def _():
            pltpu.make_async_copy(near[kind].at[:, head_columns(h, SPAN)], dealt.at[slot], recv_sem.at[0]).start()

    for fetch in fetch_order:
        fetch.wait()

    spot = lax.broadcasted_iota(jnp.int32, (blocks, blocks), 0)
    across = lax.broadcasted_iota(jnp.int32, (blocks, blocks), 1)
    order_col = jnp.sum(jnp.where(spot == across, order_row[...], 0), axis=1, keepdims=True)
    place_row[...] = jnp.max(jnp.where(order_col == across, spot, 0), axis=0, keepdims=True)
    fetch_place = pltpu.make_async_copy(place_row, place, local_sem.at[7])
    fetch_place.start()

    await_bytes(dealt, recv_sem.at[0])

    halves = dealt[...].astype(f32).reshape(PLANE, 2, 2, 8, SPAN)
    for half in range(2):
        spread[half] = halves[:, :, half].reshape(PLANE, 16, SPAN).astype(bf16)

    def own_plane(there):
        return pl.ds(there * PLANE, PLANE)

    def send_spread(d):
        there = lax.rem(y + d, ny)
        remote(spread.at[lax.rem(there, 2)], r1.at[own_plane(y)], 1, {"ctx": there * PLANE + zx}).start()

    for_each(1, ny, lambda k: send_spread(far_plane(k)))
    r1[own_plane(y)] = spread[lax.rem(y, 2)]

    def send_q(d):
        g = lax.rem(h + d, HEADS)
        remote(q_ref.at[:, head_columns(g, wide)], q_loc.at[own_rows(h), :], 2, {"head": g}).start()

    for_each(1, HEADS, lambda k: send_q(far_first(k)))
    for fetch in fetch_rest:
        fetch.wait()
    fetch_place.wait()

    lane = lax.broadcasted_iota(jnp.int32, (SPAN, SPAN), 1)
    diagonal = lane == lax.broadcasted_iota(jnp.int32, (SPAN, SPAN), 0)
    first_half = lane[:1] < BLOCK
    b0, b1 = order[0, 2 * c], order[0, 2 * c + 1]
    line0 = seg_ref[pl.ds(b0 // 2, 1), :]
    line1 = seg_ref[pl.ds(b1 // 2, 1), :]
    line0 = jnp.where(lax.rem(b0, 2) == 0, line0, jnp.concatenate([line0[:, BLOCK:], line0[:, :BLOCK]], axis=1))
    line1 = jnp.where(lax.rem(b1, 2) == 1, line1, jnp.concatenate([line1[:, BLOCK:], line1[:, :BLOCK]], axis=1))
    label_row = jnp.where(first_half, line0, line1)
    label_col = jnp.sum(jnp.where(diagonal, label_row, 0), axis=1, keepdims=True)

    def count_lower(r, count):
        return count + jnp.where(seg_ref[pl.ds(r, 1), :] < label_col, 1, 0)

    count = lax.fori_loop(0, nc, count_lower, jnp.zeros((SPAN, SPAN), jnp.int32))
    start_col = jnp.sum(count, axis=1, keepdims=True)
    start_row = jnp.sum(jnp.where(diagonal, start_col, 0), axis=0, keepdims=True)
    swapped = jnp.concatenate([start_row[:, BLOCK:], start_row[:, :BLOCK]], axis=1)
    shape4 = (PIECES, SEEN, 8, SPAN)
    key_place = (
        lax.broadcasted_iota(jnp.int32, shape4, 0) * 8
        + lax.broadcasted_iota(jnp.int32, shape4, 1) * BLOCK
        + lax.broadcasted_iota(jnp.int32, shape4, 2)
    ).reshape(WINDOW, SPAN)
    high = BACK * BLOCK + jnp.where(first_half, lane[:1], lane[:1] - BLOCK)
    for i, b in enumerate((b0, b1)):
        both = jnp.where(first_half, start_row, swapped) if i == 0 else jnp.where(first_half, swapped, start_row)
        low = both - (b - BACK) * BLOCK
        bias[i] = jnp.where((key_place >= low) & (key_place <= high), 0.0, NEVER)

    def find_slot(b, _):
        s = place[0, b]
        j = s // 2
        slots[0, b] = jnp.where(j // CLASSES == c // CLASSES, rank_of(j) * 2 + lax.rem(s, 2), 2 * CLASSES)
        return 0

    lax.fori_loop(0, blocks, find_slot, 0)

    for i in range(2):
        for head in range(GROUP):
            part = do_ref[i * BLOCK : (i + 1) * BLOCK, head * SPAN : (head + 1) * SPAN].astype(f32)
            dot_t[i, :, head * BLOCK : (head + 1) * BLOCK] = part.T

    await_bytes(r1.at[pl.ds(0, (ny - 1) * PLANE)], recv_sem.at[1])
    stored[...] = r1[...].astype(f32).reshape(blocks, 8, SPAN)
    seq[pl.ds(0, BACK)] = jnp.zeros((BACK, 8, SPAN), f32)

    def to_sequence(b, _):
        seq[b + BACK] = stored[place[0, b]]
        return 0

    lax.fori_loop(0, blocks, to_sequence, 0, unroll=8)
    first, second = pl.ds(0, PART + 8), pl.ds(PART + 8, PART - 8)

    def first_of(j):
        both = [seq[pl.ds(order[0, 2 * j], SEEN)], seq[pl.ds(order[0, 2 * j + 1], 1)]]
        return jnp.concatenate(both, axis=0).reshape(PART + 8, SPAN).astype(bf16)

    def second_of(j):
        return seq[pl.ds(order[0, 2 * j + 1] + 1, SEEN - 1)].reshape(PART - 8, SPAN).astype(bf16)

    def send_first(e):
        j = member(c, e)
        s2[e, first, :] = first_of(j)
        remote(s2.at[e, first, :], r2.at[rank_of(c), first, :], 3, {"ctx": j}).start()

    def send_second(e):
        j = member(c, e)
        s2[e, second, :] = second_of(j)
        remote(s2.at[e, second, :], r2.at[rank_of(c), second, :], 8, {"ctx": j}).start()

    for_each(1, CLASSES, lambda k: send_first(CLASSES - k))
    for_each(1, CLASSES, lambda k: send_second(CLASSES - k))
    r2[rank_of(c), first, :] = first_of(c)
    r2[rank_of(c), second, :] = second_of(c)
    peers = pl.ds(0, CLASSES - 1)
    some = pl.ds(0, (HEADS - 1) * rows)

    early, late = pl.ds(0, PART - 8), pl.ds(PART - 8, PART + 8)
    scale = SPAN ** (-0.5)
    power = scale * float(np.log2(np.e))
    for i in range(2):
        await_bytes(r2.at[peers, (first, second)[i], :], recv_sem.at[(3, 8)[i]])
        for kind, target in enumerate((keys, vals)):
            for piece in range(PIECES):
                near = r2[kind * PIECES + piece, i * (PART - 8) : i * (PART - 8) + PART + 8, :].astype(f32)
                target[i, piece * PART : (piece + 1) * PART, :] = near[8 * i : 8 * i + PART]
        if i == 0:
            await_bytes(q_loc.at[some, :], recv_sem.at[2])
        key_tile, value_tile = keys[i].astype(bf16), vals[i].astype(bf16)
        block = pl.ds(i * BLOCK, BLOCK)
        heads = range(GROUP)
        query = jnp.concatenate([q_loc[block, a * SPAN : (a + 1) * SPAN] for a in heads], axis=0)
        cotangent = jnp.concatenate([do_ref[block, a * SPAN : (a + 1) * SPAN] for a in heads], axis=0)
        scores = lax.dot_general(key_tile, query, NT, preferred_element_type=f32)
        scores = scores + jnp.concatenate([bias[i]] * (GROUP * BLOCK // SPAN), axis=1)
        top = jnp.max(scores, axis=0, keepdims=True)
        raised = jnp.exp2((scores - top) * power)
        total = jnp.sum(raised, axis=0, keepdims=True)
        sums = lax.dot_general(value_tile, raised.astype(bf16), TN, preferred_element_type=f32)
        inverse = 1.0 / total
        attended = (sums * inverse).astype(bf16).astype(f32)
        dsum = jnp.sum(dot_t[i] * attended, axis=0, keepdims=True)
        prob = raised * inverse
        vals[i] = jnp.dot(prob.astype(bf16), cotangent, preferred_element_type=f32)
        dprob = lax.dot_general(value_tile, cotangent, NT, preferred_element_type=f32)
        dscore = (prob * (dprob - dsum)).astype(bf16)
        dscores[...] = dscore
        keys[i] = jnp.dot(dscore, query, preferred_element_type=f32) * scale

        part, which = ((early, 4), (late, 9))[i]
        for kind, source in enumerate((keys, vals)):
            for piece in range(PIECES):
                mine = source[i, piece * PART : (piece + 1) * PART, :]
                if i == 0:
                    s3[kind * PIECES + piece, early, :] = mine[: PART - 8].astype(bf16)
                else:
                    before = source[0, piece * PART + PART - 8 : (piece + 1) * PART, :]
                    s3[kind * PIECES + piece, late, :] = jnp.concatenate([before, mine], axis=0).astype(bf16)

        def send_back(e):
            j = member(c, e)
            remote(s3.at[rank_of(j), part, :], r3.at[rank_of(c), part, :], which, {"ctx": j}).start()

        for_each(1, CLASSES, lambda k: send_back(CLASSES - k))
        r3[rank_of(c), part, :] = s3[rank_of(c), part, :]

        query_grad = lax.dot_general(key_tile, dscores[...], TN, preferred_element_type=f32) * scale
        attended_rows = attended.T.astype(bf16)
        query_grad_rows = query_grad.T.astype(bf16)
        for a in heads:
            att_out[block, a * SPAN : (a + 1) * SPAN] = attended_rows[a * BLOCK : (a + 1) * BLOCK]
            dq_loc[block, a * SPAN : (a + 1) * SPAN] = query_grad_rows[a * BLOCK : (a + 1) * BLOCK]

    await_bytes(r3.at[peers, early, :], recv_sem.at[4])
    await_bytes(r3.at[peers, late, :], recv_sem.at[9])
    r3f[pl.ds(0, 2 * CLASSES)] = r3[...].astype(f32).reshape(2 * CLASSES, SEEN, 8, SPAN)
    r3f[2 * CLASSES] = jnp.zeros((SEEN, 8, SPAN), f32)

    def add_up(b, sums):
        new = r3f[slots[0, b]]
        sums = [sums[k] + new[k] for k in range(SEEN)]
        acc[b] = sums[0]
        return tuple(sums[1:]) + (jnp.zeros((8, SPAN), f32),)

    sums = lax.fori_loop(0, blocks, add_up, tuple(jnp.zeros((8, SPAN), f32) for _ in range(SEEN)), unroll=4)
    for k in range(BACK):
        acc[blocks + k] = sums[k]

    def tiles_of(there):
        tiles = []
        for n in range(PLANE):
            both = [acc[order[0, 2 * (there * PLANE + n) + i] + BACK] for i in range(2)]
            tiles.append(jnp.concatenate(both, axis=0).astype(bf16))
        return jnp.stack(tiles)

    def send_sums(d):
        there = lax.rem(y + d, ny)
        s4[there] = tiles_of(there)
        remote(s4.at[there], r4.at[y], 6, {"ctx": there * PLANE + zx}).start()

    for_each(1, ny, lambda k: send_sums(far_plane(k)))
    r4[y] = tiles_of(y)

    def send_dq(d):
        g = lax.rem(h + d, HEADS)
        remote(dq_loc.at[own_rows(g), :], dq_out.at[:, head_columns(h, wide)], 5, {"head": g}).start()

    for_each(1, HEADS, lambda k: send_dq(far_first(k)))
    dq_out[:, head_columns(h, wide)] = dq_loc[own_rows(h), :]

    await_bytes(r4.at[pl.ds(0, ny - 1)], recv_sem.at[6])
    parts = []
    for half in range(2):
        part = r4[half].astype(f32)
        for there in range(half + 2, ny, 2):
            part = part + r4[there].astype(f32)
        parts.append(part.reshape(2 * PLANE, 8, SPAN))
    summed[...] = jnp.concatenate(parts, axis=1).astype(bf16)

    for kind, out in enumerate((dk_out, dv_out)):

        def send_sum(d):
            n, half = lax.rem(zx + d // 2, PLANE), lax.rem(d, 2)
            remote(
                summed.at[2 * n + half], out.at[:, head_columns(h, SPAN)], 7,
                {"ctx": y * PLANE + n, "head": half * LINE + x},
            ).start()

        @pl.when(z == kind)
        def _():
            for_each(0, 12, lambda k: send_sum(2 * (2 + k // 4 - 3 * (k // 8)) + 8 * lax.rem(k // 2, 2) + lax.rem(k, 2)))
            for_each(8, 10, send_sum)
            for half in range(2):

                @pl.when(half * LINE + x != h)
                def _():
                    send_sum(half)

                @pl.when(half * LINE + x == h)
                def _():
                    pltpu.make_async_copy(
                        summed.at[2 * zx + half], out.at[:, head_columns(h, SPAN)], recv_sem.at[7]
                    ).start()

    await_bytes(q_loc.at[some, :], recv_sem.at[5])
    await_bytes(dealt, recv_sem.at[7])
    await_bytes(r1.at[pl.ds(0, (ny - 1) * PLANE)], send_sem.at[1])
    await_bytes(q_loc.at[some, :], send_sem.at[2])
    await_bytes(r2.at[peers, first, :], send_sem.at[3])
    await_bytes(r2.at[peers, second, :], send_sem.at[8])
    await_bytes(r3.at[peers, early, :], send_sem.at[4])
    await_bytes(r3.at[peers, late, :], send_sem.at[9])
    await_bytes(q_loc.at[some, :], send_sem.at[5])
    await_bytes(r4.at[pl.ds(0, ny - 1)], send_sem.at[6])
    for which in (0, 7):

        @pl.when(own_deal)
        def _():
            await_bytes(dealt.at[pl.ds(0, 2 * PLANE - 1)], send_sem.at[which])

        @pl.when(jnp.logical_not(own_deal))
        def _():
            await_bytes(dealt, send_sem.at[which])


def put(*refs):
    sems = refs[-1]
    copies = [pltpu.make_async_copy(a, b, sems.at[i]) for i, (a, b) in enumerate(zip(refs[:4], refs[4:8]))]
    for copy in copies:
        copy.start()
    for copy in copies:
        copy.wait()


def shards(queries, keys, values, output_gradient, segment_ids, block_order):
    nc = lax.axis_size("ctx")
    wide, blocks = GROUP * SPAN, 2 * nc
    bf16, f32, i32 = jnp.bfloat16, jnp.float32, jnp.int32
    vmem = pl.BlockSpec(memory_space=pltpu.VMEM)
    anywhere = pl.BlockSpec(memory_space=pl.ANY)
    shapes = (
        jax.ShapeDtypeStruct((2 * BLOCK, wide), bf16),
        jax.ShapeDtypeStruct(queries.shape, bf16),
        jax.ShapeDtypeStruct(keys.shape, bf16),
        jax.ShapeDtypeStruct(values.shape, bf16),
    )
    results = pl.pallas_call(
        functools.partial(kernel, nc),
        out_shape=shapes,
        in_specs=[anywhere] * 6,
        out_specs=(vmem, vmem, vmem, vmem),
        scratch_shapes=[
            pltpu.VMEM((2 * BLOCK, wide), bf16),
            pltpu.VMEM((2 * PLANE, 16, SPAN), bf16),
            pltpu.VMEM((2, PLANE, 16, SPAN), bf16),
            pltpu.VMEM((nc, 16, SPAN), bf16),
            pltpu.VMEM((blocks, 8, SPAN), f32),
            pltpu.VMEM((blocks + BACK, 8, SPAN), f32),
            pltpu.VMEM((CLASSES, 2 * PART, SPAN), bf16),
            pltpu.VMEM((CLASSES, 2 * PART, SPAN), bf16),
            pltpu.VMEM((2, WINDOW, SPAN), f32),
            pltpu.VMEM((2, WINDOW, SPAN), f32),
            pltpu.VMEM((2, SPAN, GROUP * BLOCK), f32),
            pltpu.VMEM((2, WINDOW, SPAN), f32),
            pltpu.VMEM((WINDOW, GROUP * BLOCK), bf16),
            pltpu.VMEM((2 * BLOCK, wide), bf16),
            pltpu.VMEM((CLASSES, 2 * PART, SPAN), bf16),
            pltpu.VMEM((CLASSES, 2 * PART, SPAN), bf16),
            pltpu.VMEM((2 * CLASSES + 1, SEEN, 8, SPAN), f32),
            pltpu.VMEM((blocks + BACK, 8, SPAN), f32),
            pltpu.VMEM((nc // PLANE, PLANE, 16, SPAN), bf16),
            pltpu.VMEM((nc // PLANE, PLANE, 16, SPAN), bf16),
            pltpu.VMEM((2 * PLANE, 16, SPAN), bf16),
            pltpu.VMEM(keys.shape, bf16),
            pltpu.VMEM(values.shape, bf16),
            pltpu.VMEM((2 * BLOCK, wide), bf16),
            pltpu.VMEM((nc, 2 * BLOCK), i32),
            pltpu.VMEM((1, blocks), i32),
            pltpu.VMEM((1, blocks), i32),
            pltpu.SMEM((1, blocks), i32),
            pltpu.SMEM((1, blocks), i32),
            pltpu.SMEM((1, blocks), i32),
            pltpu.SemaphoreType.DMA((10,)),
            pltpu.SemaphoreType.DMA((10,)),
            pltpu.SemaphoreType.DMA((8,)),
        ],
        compiler_params=pltpu.CompilerParams(
            collective_id=0, has_side_effects=True, vmem_limit_bytes=48 * 1024 * 1024
        ),
    )(*(pltpu.with_memory_space_constraint(a, pltpu.HBM) for a in (block_order.reshape(1, blocks), queries, keys, values, output_gradient, segment_ids.reshape(nc, 2 * BLOCK))))
    return pl.pallas_call(
        put,
        out_shape=shapes,
        in_specs=[vmem] * 4,
        out_specs=(pl.BlockSpec(memory_space=pltpu.HBM),) * 4,
        scratch_shapes=[pltpu.SemaphoreType.DMA((4,))],
    )(*(pltpu.with_memory_space_constraint(a, pltpu.VMEM) for a in results))


def solution(mesh):
    in_specs = (
        P(("ctx", "head"), None),
        P(("ctx", "head"), None),
        P(("ctx", "head"), None),
        P("ctx", "head"),
        P(),
        P(),
    )
    out_specs = (
        P("ctx", "head"),
        P(("ctx", "head"), None),
        P(("ctx", "head"), None),
        P(("ctx", "head"), None),
    )
    return jax.shard_map(shards, mesh=mesh, in_specs=in_specs, out_specs=out_specs, check_vma=False)
```

```python
import functools

import jax
import jax.numpy as jnp
import numpy as np
from jax import lax
from jax.experimental import pallas as pl
from jax.experimental.pallas import tpu as pltpu
from jax.sharding import PartitionSpec as P

SPAN = 128
BLOCK = 64
GROUP = 8
BACK = 8
SEEN = BACK + 1
WINDOW = SEEN * BLOCK
LINE = 4
PAIR = 2
PLANE = LINE * PAIR
HEADS = 8
CLASSES = 16
PIECES = 8
PART = SEEN * 8
NEVER = -1e30

MESH = pl.DeviceIdType.MESH
NT = (((1,), (1,)), ((), ()))
TN = (((0,), (0,)), ((), ()))


def rank_of(c):
    return lax.rem(c // LINE, PAIR) * PIECES + lax.rem(c, LINE) * 2 + lax.rem(c // PLANE, 2)


def member(c, e):
    x = lax.rem(lax.rem(c, LINE) + lax.rem(e, LINE), LINE)
    z = lax.rem(lax.rem(c // LINE, PAIR) + lax.rem(e // LINE, PAIR), PAIR)
    y = lax.rem(lax.rem(c // PLANE, 2) + e // PLANE, 2)
    return (c // CLASSES) * CLASSES + (y * PAIR + z) * LINE + x


def await_bytes(ref, sem):
    pltpu.make_async_copy(ref, ref, sem).wait()


def kernel(
    nc,
    order_hbm, q_ref, k_ref, v_ref, do_hbm, seg_hbm,
    att_out, dq_out, dk_out, dv_out,
    q_loc, dealt, spread, r1, stored, seq, s2, r2, keys, vals, dot_t, bias,
    dscores, dq_loc, s3, r3, r3f, acc, s4, r4, summed,
    k_near, v_near, do_ref, seg_ref, order_row, place_row, order, place, slots,
    send_sem, recv_sem, local_sem,
):
    c = lax.axis_index("ctx")
    h = lax.axis_index("head")
    y, z, x, zx = c // PLANE, lax.rem(c // LINE, PAIR), lax.rem(c, LINE), lax.rem(c, PLANE)
    ny = nc // PLANE
    rows = q_ref.shape[0]
    wide = GROUP * SPAN
    blocks = 2 * nc
    f32, bf16 = jnp.float32, jnp.bfloat16
    own_deal = x == lax.rem(h, LINE)

    def remote(src, dst, which, where):
        return pltpu.make_async_remote_copy(
            src_ref=src, dst_ref=dst, send_sem=send_sem.at[which], recv_sem=recv_sem.at[which],
            device_id=where, device_id_type=MESH,
        )

    def far_first(k):
        return 4 + (k // 2) * (1 - 2 * lax.rem(k, 2))

    def for_each(low, high, what):
        def step(d, _):
            what(d)
            return 0

        lax.fori_loop(low, high, step, 0, unroll=True)

    def far_plane(k):
        return ny // 2 + (k // 2) * (1 - 2 * lax.rem(k, 2))

    barrier = pltpu.get_barrier_semaphore()

    def greet(where):
        pl.semaphore_signal(barrier, inc=1, device_id=where, device_id_type=MESH)

    def greet_dealer(d):
        greet({"ctx": y * PLANE + lax.rem(zx + d // 2, PLANE), "head": x + LINE * lax.rem(d, 2)})

    fetch_kv = [
        pltpu.make_async_copy(source, near, local_sem.at[kind])
        for kind, (source, near) in enumerate(((k_ref, k_near), (v_ref, v_near)))
    ]
    for fetch in fetch_kv:
        fetch.start()
    for_each(2, 2 * PLANE, lambda k: greet_dealer(2 * PLANE + 1 - k))
    for half in range(2):

        @pl.when(x + LINE * half != h)
        def _():
            greet({"ctx": c, "head": x + LINE * half})

    for_each(1, ny, lambda k: greet({"ctx": lax.rem(c + far_plane(k) * PLANE, nc)}))
    for_each(1, HEADS, lambda k: greet({"head": lax.rem(h + far_first(k), HEADS)}))
    for_each(1, CLASSES, lambda k: greet({"ctx": member(c, CLASSES - k)}))

    def own_rows(g):
        return pl.ds(pl.multiple_of(g * rows, rows), rows)

    def head_columns(g, width):
        return pl.ds(pl.multiple_of(g * width, width), width)

    fetch_order = [
        pltpu.make_async_copy(order_hbm, order, local_sem.at[2]),
        pltpu.make_async_copy(order_hbm, order_row, local_sem.at[3]),
    ]
    fetch_rest = [
        pltpu.make_async_copy(seg_hbm, seg_ref, local_sem.at[4]),
        pltpu.make_async_copy(do_hbm, do_ref, local_sem.at[5]),
        pltpu.make_async_copy(q_ref.at[:, head_columns(h, wide)], q_loc.at[own_rows(h), :], local_sem.at[6]),
    ]
    for fetch in fetch_order + fetch_rest:
        fetch.start()
    for fetch in fetch_kv:
        fetch.wait()
    others = 2 * PLANE + CLASSES - 1 + ny - 1 + HEADS - 1

    @pl.when(own_deal)
    def _():
        pl.semaphore_wait(barrier, others - 1)

    @pl.when(jnp.logical_not(own_deal))
    def _():
        pl.semaphore_wait(barrier, others)

    slot = zx * 2 + h // LINE
    near = (k_near, v_near)

    def deal(kind, d):
        g = lax.rem(h + d, HEADS)
        there = (y * PAIR + kind) * LINE + lax.rem(h, LINE)
        remote(near[kind].at[:, head_columns(g, SPAN)], dealt.at[slot], 0, {"ctx": there, "head": g}).start()

    def deal_both(k):
        deal(0, far_first(k))
        deal(1, far_first(k))

    for_each(1, HEADS, deal_both)
    for kind in range(2):
        stays = own_deal & (z == kind)

        @pl.when(jnp.logical_not(stays))
        def _():
            deal(kind, 0)

        @pl.when(stays)
        def _():
            pltpu.make_async_copy(near[kind].at[:, head_columns(h, SPAN)], dealt.at[slot], recv_sem.at[0]).start()

    for fetch in fetch_order:
        fetch.wait()

    spot = lax.broadcasted_iota(jnp.int32, (blocks, blocks), 0)
    across = lax.broadcasted_iota(jnp.int32, (blocks, blocks), 1)
    order_col = jnp.sum(jnp.where(spot == across, order_row[...], 0), axis=1, keepdims=True)
    place_row[...] = jnp.max(jnp.where(order_col == across, spot, 0), axis=0, keepdims=True)
    fetch_place = pltpu.make_async_copy(place_row, place, local_sem.at[7])
    fetch_place.start()

    await_bytes(dealt, recv_sem.at[0])

    halves = dealt[...].astype(f32).reshape(PLANE, 2, 2, 8, SPAN)
    for half in range(2):
        spread[half] = halves[:, :, half].reshape(PLANE, 16, SPAN).astype(bf16)

    def own_plane(there):
        return pl.ds(there * PLANE, PLANE)

    def send_spread(d):
        there = lax.rem(y + d, ny)
        remote(spread.at[lax.rem(there, 2)], r1.at[own_plane(y)], 1, {"ctx": there * PLANE + zx}).start()

    for_each(1, ny, lambda k: send_spread(far_plane(k)))
    r1[own_plane(y)] = spread[lax.rem(y, 2)]

    def send_q(d):
        g = lax.rem(h + d, HEADS)
        remote(q_ref.at[:, head_columns(g, wide)], q_loc.at[own_rows(h), :], 2, {"head": g}).start()

    for_each(1, HEADS, lambda k: send_q(far_first(k)))
    for fetch in fetch_rest:
        fetch.wait()
    fetch_place.wait()

    lane = lax.broadcasted_iota(jnp.int32, (SPAN, SPAN), 1)
    diagonal = lane == lax.broadcasted_iota(jnp.int32, (SPAN, SPAN), 0)
    first_half = lane[:1] < BLOCK
    b0, b1 = order[0, 2 * c], order[0, 2 * c + 1]
    line0 = seg_ref[pl.ds(b0 // 2, 1), :]
    line1 = seg_ref[pl.ds(b1 // 2, 1), :]
    line0 = jnp.where(lax.rem(b0, 2) == 0, line0, jnp.concatenate([line0[:, BLOCK:], line0[:, :BLOCK]], axis=1))
    line1 = jnp.where(lax.rem(b1, 2) == 1, line1, jnp.concatenate([line1[:, BLOCK:], line1[:, :BLOCK]], axis=1))
    label_row = jnp.where(first_half, line0, line1)
    label_col = jnp.sum(jnp.where(diagonal, label_row, 0), axis=1, keepdims=True)

    def count_lower(r, count):
        return count + jnp.where(seg_ref[pl.ds(r, 1), :] < label_col, 1, 0)

    count = lax.fori_loop(0, nc, count_lower, jnp.zeros((SPAN, SPAN), jnp.int32))
    start_col = jnp.sum(count, axis=1, keepdims=True)
    start_row = jnp.sum(jnp.where(diagonal, start_col, 0), axis=0, keepdims=True)
    swapped = jnp.concatenate([start_row[:, BLOCK:], start_row[:, :BLOCK]], axis=1)
    shape4 = (PIECES, SEEN, 8, SPAN)
    key_place = (
        lax.broadcasted_iota(jnp.int32, shape4, 0) * 8
        + lax.broadcasted_iota(jnp.int32, shape4, 1) * BLOCK
        + lax.broadcasted_iota(jnp.int32, shape4, 2)
    ).reshape(WINDOW, SPAN)
    high = BACK * BLOCK + jnp.where(first_half, lane[:1], lane[:1] - BLOCK)
    for i, b in enumerate((b0, b1)):
        both = jnp.where(first_half, start_row, swapped) if i == 0 else jnp.where(first_half, swapped, start_row)
        low = both - (b - BACK) * BLOCK
        bias[i] = jnp.where((key_place >= low) & (key_place <= high), 0.0, NEVER)

    def find_slot(b, _):
        s = place[0, b]
        j = s // 2
        slots[0, b] = jnp.where(j // CLASSES == c // CLASSES, rank_of(j) * 2 + lax.rem(s, 2), 2 * CLASSES)
        return 0

    lax.fori_loop(0, blocks, find_slot, 0)

    for i in range(2):
        for head in range(GROUP):
            part = do_ref[i * BLOCK : (i + 1) * BLOCK, head * SPAN : (head + 1) * SPAN].astype(f32)
            dot_t[i, :, head * BLOCK : (head + 1) * BLOCK] = part.T

    await_bytes(r1.at[pl.ds(0, (ny - 1) * PLANE)], recv_sem.at[1])
    stored[...] = r1[...].astype(f32).reshape(blocks, 8, SPAN)
    seq[pl.ds(0, BACK)] = jnp.zeros((BACK, 8, SPAN), f32)

    def to_sequence(b, _):
        seq[b + BACK] = stored[place[0, b]]
        return 0

    lax.fori_loop(0, blocks, to_sequence, 0, unroll=8)
    first, second = pl.ds(0, PART + 8), pl.ds(PART + 8, PART - 8)

    def first_of(j):
        both = [seq[pl.ds(order[0, 2 * j], SEEN)], seq[pl.ds(order[0, 2 * j + 1], 1)]]
        return jnp.concatenate(both, axis=0).reshape(PART + 8, SPAN).astype(bf16)

    def second_of(j):
        return seq[pl.ds(order[0, 2 * j + 1] + 1, SEEN - 1)].reshape(PART - 8, SPAN).astype(bf16)

    def send_first(e):
        j = member(c, e)
        s2[e, first, :] = first_of(j)
        remote(s2.at[e, first, :], r2.at[rank_of(c), first, :], 3, {"ctx": j}).start()

    def send_second(e):
        j = member(c, e)
        s2[e, second, :] = second_of(j)
        remote(s2.at[e, second, :], r2.at[rank_of(c), second, :], 8, {"ctx": j}).start()

    for_each(1, CLASSES, lambda k: send_first(CLASSES - k))
    for_each(1, CLASSES, lambda k: send_second(CLASSES - k))
    r2[rank_of(c), first, :] = first_of(c)
    r2[rank_of(c), second, :] = second_of(c)
    peers = pl.ds(0, CLASSES - 1)
    some = pl.ds(0, (HEADS - 1) * rows)

    early, late = pl.ds(0, PART - 8), pl.ds(PART - 8, PART + 8)
    scale = SPAN ** (-0.5)
    power = scale * float(np.log2(np.e))
    for i in range(2):
        await_bytes(r2.at[peers, (first, second)[i], :], recv_sem.at[(3, 8)[i]])
        tiles = []
        for kind in range(2):
            pieces = [
                r2[kind * PIECES + piece, i * (PART - 8) : i * (PART - 8) + PART + 8, :].astype(f32)[8 * i : 8 * i + PART]
                for piece in range(PIECES)
            ]
            tiles.append(jnp.concatenate(pieces, axis=0).astype(bf16))
        if i == 0:
            await_bytes(q_loc.at[some, :], recv_sem.at[2])
        key_tile, value_tile = tiles
        block = pl.ds(i * BLOCK, BLOCK)
        heads = range(GROUP)
        query = jnp.concatenate([q_loc[block, a * SPAN : (a + 1) * SPAN] for a in heads], axis=0)
        cotangent = jnp.concatenate([do_ref[block, a * SPAN : (a + 1) * SPAN] for a in heads], axis=0)
        scores = lax.dot_general(key_tile, query, NT, preferred_element_type=f32)
        scores = scores + jnp.concatenate([bias[i]] * (GROUP * BLOCK // SPAN), axis=1)
        top = jnp.max(scores, axis=0, keepdims=True)
        raised = jnp.exp2((scores - top) * power)
        total = jnp.sum(raised, axis=0, keepdims=True)
        sums = lax.dot_general(value_tile, raised.astype(bf16), TN, preferred_element_type=f32)
        inverse = 1.0 / total
        attended = (sums * inverse).astype(bf16).astype(f32)
        dsum = jnp.sum(dot_t[i] * attended, axis=0, keepdims=True)
        prob = raised * inverse
        vals[i] = jnp.dot(prob.astype(bf16), cotangent, preferred_element_type=f32)
        dprob = lax.dot_general(value_tile, cotangent, NT, preferred_element_type=f32)
        dscore = (prob * (dprob - dsum)).astype(bf16)
        dscores[...] = dscore
        keys[i] = jnp.dot(dscore, query, preferred_element_type=f32) * scale

        part, which = ((early, 4), (late, 9))[i]
        for kind, source in enumerate((keys, vals)):
            for piece in range(PIECES):
                mine = source[i, piece * PART : (piece + 1) * PART, :]
                if i == 0:
                    s3[kind * PIECES + piece, early, :] = mine[: PART - 8].astype(bf16)
                else:
                    before = source[0, piece * PART + PART - 8 : (piece + 1) * PART, :]
                    s3[kind * PIECES + piece, late, :] = jnp.concatenate([before, mine], axis=0).astype(bf16)

        def send_back(e):
            j = member(c, e)
            remote(s3.at[rank_of(j), part, :], r3.at[rank_of(c), part, :], which, {"ctx": j}).start()

        for_each(1, CLASSES, lambda k: send_back(CLASSES - k))
        r3[rank_of(c), part, :] = s3[rank_of(c), part, :]

        query_grad = lax.dot_general(key_tile, dscores[...], TN, preferred_element_type=f32) * scale
        attended_rows = attended.T.astype(bf16)
        query_grad_rows = query_grad.T.astype(bf16)
        for a in heads:
            att_out[block, a * SPAN : (a + 1) * SPAN] = attended_rows[a * BLOCK : (a + 1) * BLOCK]
            dq_loc[block, a * SPAN : (a + 1) * SPAN] = query_grad_rows[a * BLOCK : (a + 1) * BLOCK]

    await_bytes(r3.at[peers, early, :], recv_sem.at[4])
    await_bytes(r3.at[peers, late, :], recv_sem.at[9])
    r3f[pl.ds(0, 2 * CLASSES)] = r3[...].astype(f32).reshape(2 * CLASSES, SEEN, 8, SPAN)
    r3f[2 * CLASSES] = jnp.zeros((SEEN, 8, SPAN), f32)

    def add_up(b, sums):
        new = r3f[slots[0, b]]
        sums = [sums[k] + new[k] for k in range(SEEN)]
        acc[b] = sums[0]
        return tuple(sums[1:]) + (jnp.zeros((8, SPAN), f32),)

    sums = lax.fori_loop(0, blocks, add_up, tuple(jnp.zeros((8, SPAN), f32) for _ in range(SEEN)), unroll=4)
    for k in range(BACK):
        acc[blocks + k] = sums[k]

    def tiles_of(there):
        tiles = []
        for n in range(PLANE):
            both = [acc[order[0, 2 * (there * PLANE + n) + i] + BACK] for i in range(2)]
            tiles.append(jnp.concatenate(both, axis=0).astype(bf16))
        return jnp.stack(tiles)

    def send_sums(d):
        there = lax.rem(y + d, ny)
        s4[there] = tiles_of(there)
        remote(s4.at[there], r4.at[y], 6, {"ctx": there * PLANE + zx}).start()

    for_each(1, ny, lambda k: send_sums(far_plane(k)))
    r4[y] = tiles_of(y)

    def send_dq(d):
        g = lax.rem(h + d, HEADS)
        remote(dq_loc.at[own_rows(g), :], dq_out.at[:, head_columns(h, wide)], 5, {"head": g}).start()

    for_each(1, HEADS, lambda k: send_dq(far_first(k)))
    dq_out[:, head_columns(h, wide)] = dq_loc[own_rows(h), :]

    await_bytes(r4.at[pl.ds(0, ny - 1)], recv_sem.at[6])
    parts = []
    for half in range(2):
        part = r4[half].astype(f32)
        for there in range(half + 2, ny, 2):
            part = part + r4[there].astype(f32)
        parts.append(part.reshape(2 * PLANE, 8, SPAN))
    summed[...] = jnp.concatenate(parts, axis=1).astype(bf16)

    for kind, out in enumerate((dk_out, dv_out)):

        def send_sum(d):
            n, half = lax.rem(zx + d // 2, PLANE), lax.rem(d, 2)
            remote(
                summed.at[2 * n + half], out.at[:, head_columns(h, SPAN)], 7,
                {"ctx": y * PLANE + n, "head": half * LINE + x},
            ).start()

        @pl.when(z == kind)
        def _():
            for_each(0, 12, lambda k: send_sum(2 * (2 + k // 4 - 3 * (k // 8)) + 8 * lax.rem(k // 2, 2) + lax.rem(k, 2)))
            for_each(8, 10, send_sum)
            for half in range(2):

                @pl.when(half * LINE + x != h)
                def _():
                    send_sum(half)

                @pl.when(half * LINE + x == h)
                def _():
                    pltpu.make_async_copy(
                        summed.at[2 * zx + half], out.at[:, head_columns(h, SPAN)], recv_sem.at[7]
                    ).start()

    await_bytes(q_loc.at[some, :], recv_sem.at[5])
    await_bytes(dealt, recv_sem.at[7])
    await_bytes(r1.at[pl.ds(0, (ny - 1) * PLANE)], send_sem.at[1])
    await_bytes(q_loc.at[some, :], send_sem.at[2])
    await_bytes(r2.at[peers, first, :], send_sem.at[3])
    await_bytes(r2.at[peers, second, :], send_sem.at[8])
    await_bytes(r3.at[peers, early, :], send_sem.at[4])
    await_bytes(r3.at[peers, late, :], send_sem.at[9])
    await_bytes(q_loc.at[some, :], send_sem.at[5])
    await_bytes(r4.at[pl.ds(0, ny - 1)], send_sem.at[6])
    for which in (0, 7):

        @pl.when(own_deal)
        def _():
            await_bytes(dealt.at[pl.ds(0, 2 * PLANE - 1)], send_sem.at[which])

        @pl.when(jnp.logical_not(own_deal))
        def _():
            await_bytes(dealt, send_sem.at[which])


def put(*refs):
    sems = refs[-1]
    copies = [pltpu.make_async_copy(a, b, sems.at[i]) for i, (a, b) in enumerate(zip(refs[:4], refs[4:8]))]
    for copy in copies:
        copy.start()
    for copy in copies:
        copy.wait()


def shards(queries, keys, values, output_gradient, segment_ids, block_order):
    nc = lax.axis_size("ctx")
    wide, blocks = GROUP * SPAN, 2 * nc
    bf16, f32, i32 = jnp.bfloat16, jnp.float32, jnp.int32
    vmem = pl.BlockSpec(memory_space=pltpu.VMEM)
    anywhere = pl.BlockSpec(memory_space=pl.ANY)
    shapes = (
        jax.ShapeDtypeStruct((2 * BLOCK, wide), bf16),
        jax.ShapeDtypeStruct(queries.shape, bf16),
        jax.ShapeDtypeStruct(keys.shape, bf16),
        jax.ShapeDtypeStruct(values.shape, bf16),
    )
    results = pl.pallas_call(
        functools.partial(kernel, nc),
        out_shape=shapes,
        in_specs=[anywhere] * 6,
        out_specs=(vmem, vmem, vmem, vmem),
        scratch_shapes=[
            pltpu.VMEM((2 * BLOCK, wide), bf16),
            pltpu.VMEM((2 * PLANE, 16, SPAN), bf16),
            pltpu.VMEM((2, PLANE, 16, SPAN), bf16),
            pltpu.VMEM((nc, 16, SPAN), bf16),
            pltpu.VMEM((blocks, 8, SPAN), f32),
            pltpu.VMEM((blocks + BACK, 8, SPAN), f32),
            pltpu.VMEM((CLASSES, 2 * PART, SPAN), bf16),
            pltpu.VMEM((CLASSES, 2 * PART, SPAN), bf16),
            pltpu.VMEM((2, WINDOW, SPAN), f32),
            pltpu.VMEM((2, WINDOW, SPAN), f32),
            pltpu.VMEM((2, SPAN, GROUP * BLOCK), f32),
            pltpu.VMEM((2, WINDOW, SPAN), f32),
            pltpu.VMEM((WINDOW, GROUP * BLOCK), bf16),
            pltpu.VMEM((2 * BLOCK, wide), bf16),
            pltpu.VMEM((CLASSES, 2 * PART, SPAN), bf16),
            pltpu.VMEM((CLASSES, 2 * PART, SPAN), bf16),
            pltpu.VMEM((2 * CLASSES + 1, SEEN, 8, SPAN), f32),
            pltpu.VMEM((blocks + BACK, 8, SPAN), f32),
            pltpu.VMEM((nc // PLANE, PLANE, 16, SPAN), bf16),
            pltpu.VMEM((nc // PLANE, PLANE, 16, SPAN), bf16),
            pltpu.VMEM((2 * PLANE, 16, SPAN), bf16),
            pltpu.VMEM(keys.shape, bf16),
            pltpu.VMEM(values.shape, bf16),
            pltpu.VMEM((2 * BLOCK, wide), bf16),
            pltpu.VMEM((nc, 2 * BLOCK), i32),
            pltpu.VMEM((1, blocks), i32),
            pltpu.VMEM((1, blocks), i32),
            pltpu.SMEM((1, blocks), i32),
            pltpu.SMEM((1, blocks), i32),
            pltpu.SMEM((1, blocks), i32),
            pltpu.SemaphoreType.DMA((10,)),
            pltpu.SemaphoreType.DMA((10,)),
            pltpu.SemaphoreType.DMA((8,)),
        ],
        compiler_params=pltpu.CompilerParams(
            collective_id=0, has_side_effects=True, vmem_limit_bytes=48 * 1024 * 1024
        ),
    )(*(pltpu.with_memory_space_constraint(a, pltpu.HBM) for a in (block_order.reshape(1, blocks), queries, keys, values, output_gradient, segment_ids.reshape(nc, 2 * BLOCK))))
    return pl.pallas_call(
        put,
        out_shape=shapes,
        in_specs=[vmem] * 4,
        out_specs=(pl.BlockSpec(memory_space=pltpu.HBM),) * 4,
        scratch_shapes=[pltpu.SemaphoreType.DMA((4,))],
    )(*(pltpu.with_memory_space_constraint(a, pltpu.VMEM) for a in results))


def solution(mesh):
    in_specs = (
        P(("ctx", "head"), None),
        P(("ctx", "head"), None),
        P(("ctx", "head"), None),
        P("ctx", "head"),
        P(),
        P(),
    )
    out_specs = (
        P("ctx", "head"),
        P(("ctx", "head"), None),
        P(("ctx", "head"), None),
        P(("ctx", "head"), None),
    )
    return jax.shard_map(shards, mesh=mesh, in_specs=in_specs, out_specs=out_specs, check_vma=False)
```
